256 devices in a mesh: lat: 8 (over y, x_hi), lon: 32 (over x_lo, z, core).
Axes of the slice: x: 4 (x_hi: 2, x_lo: 2; x = x_hi * 2 + x_lo), y: 4, z: 8, core: 2. Of those that a mesh axis runs over, the one named last changes fastest.
Arguments:
- tokens: bfloat16 [4, 48, 768, 512], P(None, 'lat', 'lon'), may hold values from -6 to 6
- cotangent: bfloat16 [4, 48, 768, 512], P(None, 'lat', 'lon'), may hold values from -6 to 6
- w_qkv: bfloat16 [512, 1536], replicated, may hold values from -0.26516504 to 0.26516504
- w_out: bfloat16 [512, 512], replicated, may hold values from -0.25 to 0.25
- norm_gain_vector: float32 [512], replicated, may hold values from 0.1 to 1.9
Outputs:
- layer_out: bfloat16 [4, 48, 768, 512], P(None, 'lat', 'lon')
- grad_tokens: bfloat16 [4, 48, 768, 512], P(None, 'lat', 'lon')
- grad_qkv: bfloat16 [512, 1536], replicated
- grad_out: bfloat16 [512, 512], replicated
- grad_gain: float32 [512], replicated
The draws below stay inside these ranges and needn't reach their ends.
All inputs are finite; a program needn't handle non-finite values.
Results may differ from the reference program's by a relative error of at most 0.014.
Values may be sent and summed in bfloat16 or wider, within the bound.
A program may use at most 64 MiB of HBM per device.

```python
import math
import jax
import jax.numpy as jnp
from jax import lax

C = 512
HEADS = 8
LEVELS = 4
WIN_LEV = 2
WIN_LAT = 6
WIN_LON = 12
LAT = 48
LON = 768


def shared_pattern(key):
    common = jax.random.fold_in(key, 91)
    order = jax.random.permutation(jax.random.fold_in(common, 1), C)
    direction = jnp.where(order < C // 2, 1.0, -1.0).astype(jnp.float32)
    head_dim = C // HEADS
    flips = jax.random.randint(jax.random.fold_in(common, 2), (head_dim,), 0, 2)
    signs = (2 * flips - 1).astype(jnp.float32)
    chosen = jax.random.permutation(jax.random.fold_in(common, 3), HEADS)
    head_of = jnp.arange(C, dtype=jnp.int32) // head_dim
    picked = (head_of == chosen[0]) | (head_of == chosen[1])
    along = jnp.where(picked, jnp.tile(signs, HEADS), 0.0).astype(jnp.float32) / math.sqrt(head_dim)
    return (direction, along)


def draw_w_qkv(key, part):
    direction, along = shared_pattern(key)
    key = jax.random.fold_in(key, 5)
    head_dim = C // HEADS
    bound = 6.0 / math.sqrt(C)
    base = jax.random.normal(key, (C, 3 * C), jnp.float32) / math.sqrt(C)
    target = 6.0
    strength = math.sqrt(target * math.sqrt(head_dim) / C)
    rank_one = strength * (direction / math.sqrt(C))[:, None] * along[None, :]
    zeros = jnp.zeros((C, C), jnp.float32)
    planted = jnp.concatenate([rank_one, rank_one, zeros], axis=1)
    return jnp.clip(base + planted, -bound, bound).astype(jnp.bfloat16)


def draw_tokens(key, part):
    key = jax.random.fold_in(key, 7)
    shape = (LEVELS, LAT, LON, C)
    return jnp.clip(jax.random.normal(key, shape, jnp.float32), -6.0, 6.0).astype(jnp.bfloat16)


def block_levels(stream_key, shape, split, smallest, largest):
    factor_of = 1.0
    for dim, blocks in split:
        steps = jax.random.uniform(jax.random.fold_in(jax.random.fold_in(stream_key, 6), dim), (blocks,), jnp.float32, smallest / len(split), largest / len(split))
        factor_of = factor_of * jnp.repeat(jnp.exp(steps), shape[dim] // blocks).reshape((-1,) + (1,) * (len(shape) - 1 - dim))
    return factor_of


def gaussian(key, extent, width, most, pieces=(), kind=jnp.bfloat16):
    array = jax.random.normal(key, extent, jnp.float32) * width
    if len(pieces) > 0:
        array = block_levels(key, extent, pieces, -0.22, 0.18) * array
    return jnp.clip(array, min=-most, max=most).astype(kind)


def setup_inputs(seed: int = 0) -> dict:
    seeds = jax.random.split(jax.random.key(seed), 6)
    return {
        "tokens": draw_tokens(jax.random.fold_in(seeds[5], 71), 0),
        "cotangent": gaussian(seeds[1], (LEVELS, LAT, LON, C), 1.0, 6.0, ((1, 8), (2, 32))),
        "w_qkv": draw_w_qkv(jax.random.fold_in(seeds[5], 71), 0),
        "w_out": gaussian(seeds[3], (C, C), C ** -0.5, 0.25),
        "norm_gain_vector": jnp.clip(1.0 + 0.18 * jax.random.normal(seeds[4], (C,), jnp.float32), 0.1, 1.9),
    }


def to_windows(grid):
    lv, rows, cols, ch = grid.shape
    grid = grid.reshape(lv // WIN_LEV, WIN_LEV, rows // WIN_LAT, WIN_LAT, cols // WIN_LON, WIN_LON, ch)
    grid = grid.transpose(0, 2, 4, 1, 3, 5, 6)
    return grid.reshape(-1, WIN_LEV * WIN_LAT * WIN_LON, ch)

def from_windows(wins, lv, rows, cols):
    ch = wins.shape[-1]
    grid = wins.reshape(lv // WIN_LEV, rows // WIN_LAT, cols // WIN_LON, WIN_LEV, WIN_LAT, WIN_LON, ch)
    return grid.transpose(0, 3, 1, 4, 2, 5, 6).reshape(lv, rows, cols, ch)

def lift(value):
    return value.astype(jnp.float32)

def window_layer(x_win, g_win, labels, w_qkv, w_out, norm_gain_vector):
    nwin, span, ch = x_win.shape
    head_dim = ch // HEADS
    scale = head_dim ** (-0.5)
    same = labels[:, :, None] == labels[:, None, :]
    xf = x_win.astype(jnp.float32)
    centered_tokens = xf - lax.optimization_barrier(jnp.mean(xf, axis=-1, keepdims=True))
    inverse_deviation = lax.rsqrt(lax.optimization_barrier(jnp.mean(centered_tokens * centered_tokens, axis=-1, keepdims=True)) + 1e-05)
    standardized_tokens = centered_tokens * inverse_deviation
    normalized_tokens = (standardized_tokens * norm_gain_vector).astype(jnp.bfloat16)
    qkv = jnp.einsum('wsc,cf->wsf', lift(normalized_tokens), lift(w_qkv)).astype(jnp.bfloat16)
    query = qkv[:, :, :ch].reshape(nwin, span, HEADS, head_dim)
    keys = qkv[:, :, ch:2 * ch].reshape(nwin, span, HEADS, head_dim)
    values = qkv[:, :, 2 * ch:].reshape(nwin, span, HEADS, head_dim)
    scores = jnp.einsum('wshd,wthd->whst', lift(query), lift(keys)) * scale
    scores = jnp.where(same[:, None], scores, -jnp.inf)
    top = lax.optimization_barrier(jnp.max(scores, axis=-1, keepdims=True))
    expo = jnp.exp(scores - top)
    probs = expo / lax.optimization_barrier(jnp.sum(expo, axis=-1, keepdims=True))
    probs_b = probs.astype(jnp.bfloat16)
    attn = jnp.einsum('whst,wthd->wshd', lift(probs_b), lift(values)).astype(jnp.bfloat16).reshape(nwin, span, ch)
    branch = jnp.einsum('wsc,cd->wsd', lift(attn), lift(w_out)).astype(jnp.bfloat16)
    d_attn = jnp.einsum('wsd,cd->wsc', lift(g_win), lift(w_out)).astype(jnp.bfloat16)
    d_wout = jnp.einsum('wsc,wsd->cd', lift(attn), lift(g_win))
    d_heads = d_attn.reshape(nwin, span, HEADS, head_dim)
    d_probs = jnp.einsum('wshd,wthd->whst', lift(d_heads), lift(values))
    d_values = jnp.einsum('whst,wshd->wthd', lift(probs_b), lift(d_heads)).astype(jnp.bfloat16)
    d_scores = (probs * (d_probs - lax.optimization_barrier(jnp.sum(d_probs * probs, axis=-1, keepdims=True))) * scale).astype(jnp.bfloat16)
    d_query = jnp.einsum('whst,wthd->wshd', lift(d_scores), lift(keys)).astype(jnp.bfloat16)
    d_keys = jnp.einsum('whst,wshd->wthd', lift(d_scores), lift(query)).astype(jnp.bfloat16)
    d_qkv = jnp.concatenate([d_query.reshape(nwin, span, ch), d_keys.reshape(nwin, span, ch), d_values.reshape(nwin, span, ch)], axis=-1)
    d_wqkv = jnp.einsum('wsc,wsf->cf', lift(normalized_tokens), lift(d_qkv))
    normalized_gradient = jnp.einsum('wsf,cf->wsc', lift(d_qkv), lift(w_qkv))
    gain_gradient = lax.optimization_barrier(jnp.sum(normalized_gradient * standardized_tokens, axis=(0, 1)))
    standardized_gradient = normalized_gradient * norm_gain_vector
    shifted_gradient = inverse_deviation * (standardized_gradient - lax.optimization_barrier(jnp.mean(standardized_gradient, axis=-1, keepdims=True)) - standardized_tokens * lax.optimization_barrier(jnp.mean(standardized_gradient * standardized_tokens, axis=-1, keepdims=True)))
    return (branch, shifted_gradient.astype(jnp.bfloat16), d_wqkv, d_wout, gain_gradient)

def reference(tokens, cotangent, w_qkv, w_out, norm_gain_vector):
    lv, rows, cols, ch = tokens.shape
    offsets = (-(WIN_LEV // 2), -(WIN_LAT // 2), -(WIN_LON // 2))
    rolled = jnp.roll(tokens, offsets, axis=(0, 1, 2))
    rolled_grad = jnp.roll(cotangent, offsets, axis=(0, 1, 2))
    lat_label = (jnp.arange(rows, dtype=jnp.int32) >= rows - WIN_LAT // 2).astype(jnp.int32)
    lev_label = (jnp.arange(lv, dtype=jnp.int32) == lv - 1).astype(jnp.int32)
    label_grid = 2 * lat_label[None, :, None] + lev_label[:, None, None] + jnp.zeros((lv, rows, cols), jnp.int32)
    labels = to_windows(label_grid[..., None])[..., 0]
    per_block = cols // WIN_LON
    x_win = to_windows(rolled)
    g_win = to_windows(rolled_grad)
    span = x_win.shape[1]
    x_blocks = x_win.reshape(-1, per_block, span, ch)
    g_blocks = g_win.reshape(-1, per_block, span, ch)
    l_blocks = labels.reshape(-1, per_block, span)

    def step(carry, item):
        xb, gb, lb = item
        branch, shifted_gradient, d_wqkv, d_wout, gain_gradient = window_layer(xb, gb, lb, w_qkv, w_out, norm_gain_vector)
        return ((carry[0] + d_wqkv, carry[1] + d_wout, carry[2] + gain_gradient), (branch, shifted_gradient))
    init = (jnp.zeros((ch, 3 * ch), jnp.float32), jnp.zeros((ch, ch), jnp.float32), jnp.zeros((ch,), jnp.float32))
    totals, outs = lax.scan(step, init, (x_blocks, g_blocks, l_blocks))
    branch = from_windows(outs[0].reshape(-1, span, ch), lv, rows, cols)
    shifted_gradient = from_windows(outs[1].reshape(-1, span, ch), lv, rows, cols)
    back = (WIN_LEV // 2, WIN_LAT // 2, WIN_LON // 2)
    branch = jnp.roll(branch, back, axis=(0, 1, 2))
    shifted_gradient = jnp.roll(shifted_gradient, back, axis=(0, 1, 2))
    layer_out = (tokens.astype(jnp.float32) + branch.astype(jnp.float32)).astype(jnp.bfloat16)
    grad_tokens = (cotangent.astype(jnp.float32) + shifted_gradient.astype(jnp.float32)).astype(jnp.bfloat16)
    return (layer_out, grad_tokens, totals[0].astype(jnp.bfloat16), totals[1].astype(jnp.bfloat16), totals[2])
```

```python
import functools

import jax
import jax.numpy as jnp
from jax import lax
from jax.experimental import pallas as pl
from jax.experimental.pallas import tpu as pltpu
from jax.sharding import PartitionSpec as P

CH = 512
HEADS = 8
HEAD_DIM = CH // HEADS
LEVELS = 4
ROWS = 6
HALF = 3
COLS = 24
SPAN = 144
CHUNK = 144
LAST_BAND = 7
GRADS = 4 * CH
SCALE = HEAD_DIM ** (-0.5)
LOG2E = 1.4426950408889634
MASKED = -1e30
LANES = 128
MESH = pl.DeviceIdType.MESH
f32 = jnp.float32
bf16 = jnp.bfloat16


def nt(a, b):
    return lax.dot_general(a, b, (((1,), (1,)), ((), ())), preferred_element_type=f32)


def tn(a, b):
    return lax.dot_general(a, b, (((0,), (0,)), ((), ())), preferred_element_type=f32)


def nn(a, b):
    return lax.dot_general(a, b, (((1,), (0,)), ((), ())), preferred_element_type=f32)


def turned(v, by):
    by = by % COLS
    return v if by == 0 else pltpu.roll(v, by, axis=0)


def place():
    lat, lon = lax.axis_index("lat"), lax.axis_index("lon")
    y, x_hi = lat // 2, lat % 2
    x_lo, z, core = lon // 16, (lon % 16) // 2, lon % 2
    return 2 * x_hi + x_lo, y, z, core


def device_at(x, y, z, core):
    return (2 * y + x // 2, 16 * (x % 2) + 2 * z + core)


def neighbour(by_lat, by_lon):
    lat, lon = lax.axis_index("lat"), lax.axis_index("lon")
    return ((lat + by_lat + 8) % 8, (lon + by_lon + 32) % 32)


def along(dim, k):
    x, y, z, core = place()
    if dim == "x":
        return device_at((x + k) % 4, y, z, core)
    if dim == "y":
        return device_at(x, (y + k) % 4, z, core)
    if dim == "z":
        return device_at(x, y, (z + k) % 8, core)
    return device_at(x, y, z, 1 - core)


def send(src, dst, sems, slot, device):
    return pltpu.make_async_remote_copy(
        src_ref=src,
        dst_ref=dst,
        send_sem=sems[0].at[slot],
        recv_sem=sems[1].at[slot],
        device_id=device,
        device_id_type=MESH,
    )


def greet(devices):
    barrier = pltpu.get_barrier_semaphore()
    for device in devices:
        pl.semaphore_signal(barrier, inc=1, device_id=device, device_id_type=MESH)
    pl.semaphore_wait(barrier, len(devices))


def pack_half(h, first, second, packed):
    row = lax.broadcasted_iota(jnp.int32, (COLS, LANES), 0)

    def lanes_step(c, _):
        lanes = pl.ds(pl.multiple_of(c * LANES, LANES), LANES)
        kinds = [[], [], [], []]
        for src in (first, second):
            for i in range(HALF):
                v0, v1, v2, v3 = (
                    src[l, HALF * h + i, :, lanes].astype(f32) for l in range(LEVELS)
                )
                kinds[0].append(jnp.where(row < 12, turned(v1, -6), turned(v2, 6)))
                kinds[1].append(jnp.where(row < 12, turned(v3, -6), turned(v0, 6)))
                kinds[2].append(
                    jnp.where(
                        row < 12,
                        jnp.where(row < 6, turned(v1, 6), turned(v2, 12)),
                        jnp.where(row < 18, turned(v3, 18), v0),
                    )
                )
                kinds[3].append(
                    jnp.where(
                        row < 12,
                        jnp.where(row < 6, v1, turned(v2, 6)),
                        jnp.where(row < 18, turned(v3, 12), turned(v0, 18)),
                    )
                )
        for kind in range(4):
            packed[h, kind, :, lanes] = jnp.concatenate(kinds[kind], axis=0).astype(bf16)
        return 0

    lax.fori_loop(0, CH // LANES, lanes_step, 0)


def unpack_half(h, chunks, first, second, first_out, second_out):
    row = lax.broadcasted_iota(jnp.int32, (COLS, LANES), 0)

    def lanes_step(c, _):
        lanes = pl.ds(pl.multiple_of(c * LANES, LANES), LANES)
        kinds = [chunks[kind][:, lanes].astype(f32) for kind in range(4)]
        for n, (src, out) in enumerate(((first, first_out), (second, second_out))):
            for i in range(HALF):
                at = 72 * n + COLS * i
                a0, a1, b, e = (kind[at : at + COLS] for kind in kinds)
                west, east = row < 6, row >= 18
                v1 = jnp.where(west, e, jnp.where(east, turned(b, 18), turned(a0, 6)))
                v2 = jnp.where(
                    west, turned(e, 18), jnp.where(east, turned(b, 12), turned(a0, 18))
                )
                v3 = jnp.where(
                    west, turned(e, 12), jnp.where(east, turned(b, 6), turned(a1, 6))
                )
                v0 = jnp.where(west, turned(e, 6), jnp.where(east, b, turned(a1, 18)))
                for l, v in enumerate((v0, v1, v2, v3)):
                    r = HALF * h + i
                    total = src[l, r, :, lanes].astype(f32) + v
                    out[l, r, :, lanes] = total.astype(bf16)
        return 0

    lax.fori_loop(0, CH // LANES, lanes_step, 0)


def by_pair(blocks):
    row = lax.broadcasted_iota(jnp.int32, blocks[0].shape, 0)
    pairs = ([], [])
    for j in range(3):
        a, b = blocks[2 * j], blocks[2 * j + 1]
        pairs[0].append(jnp.where(row < 12, a, turned(b, 12)))
        pairs[1].append(jnp.where(row < 12, turned(a, 12), b))
    return pairs


def by_row(pairs):
    row = lax.broadcasted_iota(jnp.int32, pairs[0][0].shape, 0)
    blocks = []
    for j in range(3):
        a, b = pairs[0][j], pairs[1][j]
        blocks.append(jnp.where(row < 12, a, turned(b, 12)))
        blocks.append(jnp.where(row < 12, turned(a, 12), b))
    return blocks


def blocks_of(value, n):
    return [value[72 * n + COLS * i : 72 * n + COLS * (i + 1)] for i in range(HALF)]


def set_bias(bias):
    last = (lax.axis_index("lat") == LAST_BAND).astype(jnp.int32)
    shape = (SPAN, SPAN)
    for s in range(2):
        labels = []
        for dim in range(2):
            i = lax.broadcasted_iota(jnp.int32, shape, dim)
            if s == 0:
                lat_row = i // COLS
                level = (i % COLS) // 12
            else:
                t = i % 72
                u = t % COLS
                lat_row = 2 * (t // COLS) + u // 12
                level = (u % 12) // 6
            labels.append((last * (lat_row < HALF).astype(jnp.int32), level))
        (kr, kl), (qr, ql) = labels
        same_row = kr == qr
        bias[s, 0] = jnp.where(same_row, 0.0, MASKED).astype(f32)
        bias[s, 1] = jnp.where(same_row & (kl == ql), 0.0, MASKED).astype(f32)


def norm_block(x, gain):
    mean = jnp.mean(x, axis=-1, keepdims=True)
    centered = x - mean
    inverse = lax.rsqrt(jnp.mean(centered * centered, axis=-1, keepdims=True) + 1e-05)
    xhat = centered * inverse
    return xhat, inverse, (xhat * gain).astype(bf16)


def load_windows(s, chunk_ref, gain_ref, normed, grads, xhat_ref, inverse_ref):
    gain = gain_ref[...]
    base = 2 * SPAN * s

    def store(off, xs, gs):
        x = jnp.concatenate(xs, axis=0)
        xhat, inverse, n = norm_block(x, gain)
        xhat_ref[off : off + 48] = xhat
        inverse_ref[off : off + 48] = jnp.broadcast_to(inverse, (48, LANES))
        normed[base + off : base + off + 48] = n
        grads[base + off : base + off + 48] = jnp.concatenate(gs, axis=0).astype(bf16)

    if s == 0:
        for p in range(2):
            halves = [chunk_ref(h, p)[...].astype(f32) for h in range(2)]
            xs = sum((blocks_of(v, 0) for v in halves), [])
            gs = sum((blocks_of(v, 1) for v in halves), [])
            for j in range(3):
                store(SPAN * p + 48 * j, xs[2 * j : 2 * j + 2], gs[2 * j : 2 * j + 2])
    else:
        parts = []
        for n in range(2):
            sides = []
            for kind in (2, 3):
                halves = [chunk_ref(h, kind)[...].astype(f32) for h in range(2)]
                sides.append(by_pair(sum((blocks_of(v, n) for v in halves), [])))
            parts.append([sides[0][p] + sides[1][p] for p in range(2)])
        for p in range(2):
            for j in range(3):
                store(
                    SPAN * p + 48 * j,
                    parts[0][p][2 * j : 2 * j + 2],
                    parts[1][p][2 * j : 2 * j + 2],
                )


def head_pair(s, p, lanes_of, bias, qkv, d_attn, attn, d_qkv):
    rows = slice(SPAN * p, SPAN * (p + 1))
    base = 2 * SPAN * s + SPAN * p
    out_rows = slice(base, base + SPAN)
    q = qkv[rows, lanes_of(0)]
    k = qkv[rows, lanes_of(1)]
    v = qkv[rows, lanes_of(2)]
    g = d_attn[rows, lanes_of(0)]
    lane = lax.broadcasted_iota(jnp.int32, (SPAN, LANES), 1)
    o, dq, dk, dv = [], [], [], []
    for e in range(2):
        mine = (lane < HEAD_DIM) if e == 0 else (lane >= HEAD_DIM)
        zero = jnp.zeros((), bf16)
        qm = jnp.where(mine, q, zero)
        km = jnp.where(mine, k, zero)
        vm = jnp.where(mine, v, zero)
        gm = jnp.where(mine, g, zero)
        scores = nt(k, qm) * (SCALE * LOG2E) + bias[s, p]
        top = jnp.max(scores, axis=0, keepdims=True)
        expo = jnp.exp2(scores - top)
        probs = expo * (1.0 / jnp.sum(expo, axis=0, keepdims=True))
        probs_b = probs.astype(bf16)
        d_probs = nt(v, gm)
        mean = jnp.sum(d_probs * probs, axis=0, keepdims=True)
        d_scores = (probs * (d_probs - mean) * SCALE).astype(bf16)
        o.append(tn(probs_b, vm))
        dv.append(nn(probs_b, gm))
        dq.append(tn(d_scores, km))
        dk.append(nn(d_scores, qm))
    attn[out_rows, lanes_of(0)] = (o[0] + o[1]).astype(bf16)
    d_qkv[out_rows, lanes_of(0)] = (dq[0] + dq[1]).astype(bf16)
    d_qkv[out_rows, lanes_of(1)] = (dk[0] + dk[1]).astype(bf16)
    d_qkv[out_rows, lanes_of(2)] = (dv[0] + dv[1]).astype(bf16)


def windows(s, chunk_ref, result_ref, w, scratch):
    w_qkv, w_out, gain_ref = w
    (normed, grads, attn, d_qkv, qkv, d_attn, xhat_ref, inverse_ref, branch, shifted, bias, gain_sum) = scratch
    base = 2 * SPAN * s
    rows = slice(base, base + 2 * SPAN)
    load_windows(s, chunk_ref, gain_ref, normed, grads, xhat_ref, inverse_ref)
    for n in range(3):
        cols = slice(CH * n, CH * (n + 1))
        qkv[:, cols] = nn(normed[rows], w_qkv[:, cols]).astype(bf16)
    d_attn[...] = nt(grads[rows], w_out[...]).astype(bf16)

    def pair_step(hp, _):
        def lanes_of(n):
            return pl.ds(pl.multiple_of(CH * n + LANES * hp, LANES), LANES)

        for p in range(2):
            head_pair(s, p, lanes_of, bias, qkv, d_attn, attn, d_qkv)
        return 0

    lax.fori_loop(0, HEADS // 2, pair_step, 0)
    branch[...] = nn(attn[rows], w_out[...])
    shifted[...] = nt(d_qkv[rows], w_qkv[...])
    gain = gain_ref[...]
    for i in range(6):
        at = slice(48 * i, 48 * (i + 1))
        d_normed = shifted[at]
        xhat = xhat_ref[at]
        gain_sum[...] += jnp.sum((d_normed * xhat).reshape(6, 8, CH), axis=0)
        d_xhat = d_normed * gain
        mean = jnp.mean(d_xhat, axis=-1, keepdims=True)
        slope = jnp.mean(d_xhat * xhat, axis=-1, keepdims=True)
        shifted[at] = inverse_ref[at, 0:1] * (d_xhat - mean - xhat * slope)
    if s == 0:
        for p in range(2):
            for h in range(2):
                at = slice(SPAN * p + 72 * h, SPAN * p + 72 * (h + 1))
                result_ref(h, p)[...] = jnp.concatenate(
                    [branch[at], shifted[at]], axis=0
                ).astype(bf16)
    else:
        for side, kind in enumerate((2, 3)):
            blocks = []
            for value in (branch, shifted):
                pairs = [
                    [
                        value[SPAN * p + 72 * side + COLS * j : SPAN * p + 72 * side + COLS * (j + 1)]
                        for j in range(3)
                    ]
                    for p in range(2)
                ]
                blocks.append(by_row(pairs))
            for h in range(2):
                result_ref(h, kind)[...] = jnp.concatenate(
                    blocks[0][HALF * h : HALF * h + HALF] + blocks[1][HALF * h : HALF * h + HALF],
                    axis=0,
                ).astype(bf16)


def weight_grads(n, total, scratch):
    normed, grads, attn, d_qkv = scratch[:4]
    cols = slice(CH * n, CH * (n + 1))
    if n < 3:
        total[:, cols] = tn(normed[...], d_qkv[:, cols]).astype(bf16)
    else:
        total[:, cols] = tn(attn[...], grads[...]).astype(bf16)


def gain_rows(gain_sum, gain_out):
    row = jnp.sum(gain_sum[...], axis=0, keepdims=True)
    gain_out[...] = jnp.concatenate(
        [row[:, LANES * i : LANES * (i + 1)] for i in range(4)] + [jnp.zeros((4, LANES), f32)],
        axis=0,
    )


WINDOW_SCRATCH = [
    pltpu.VMEM((4 * SPAN, CH), bf16),
    pltpu.VMEM((4 * SPAN, CH), bf16),
    pltpu.VMEM((4 * SPAN, CH), bf16),
    pltpu.VMEM((4 * SPAN, 3 * CH), bf16),
    pltpu.VMEM((2 * SPAN, 3 * CH), bf16),
    pltpu.VMEM((2 * SPAN, CH), bf16),
    pltpu.VMEM((2 * SPAN, CH), f32),
    pltpu.VMEM((2 * SPAN, LANES), f32),
    pltpu.VMEM((2 * SPAN, CH), f32),
    pltpu.VMEM((2 * SPAN, CH), f32),
    pltpu.VMEM((2, 2, SPAN, SPAN), f32),
    pltpu.VMEM((8, CH), f32),
]


def compute_kernel(work, w_qkv, w_out, gain, result, total, gain_out, *scratch):
    set_bias(scratch[10])
    scratch[11][...] = jnp.zeros((8, CH), f32)
    for s in range(2):
        windows(
            s,
            lambda h, kind: work.at[h, kind],
            lambda h, kind: result.at[h, kind],
            (w_qkv, w_out, gain),
            scratch,
        )
    gain_rows(scratch[11], gain_out)
    for n in range(4):
        weight_grads(n, total, scratch)


FLOWS = (("x", "y"), ("y", "x"))
FLOW_COLS = GRADS // 2


def partners():
    return (
        [along("core", 0)]
        + [along("x", k) for k in (1, 2, 3)]
        + [along("y", k) for k in (1, 2, 3)]
        + [along("z", k) for k in range(1, 8)]
    )


SUM_SCRATCH = [
    pltpu.VMEM((256, GRADS), bf16),
    pltpu.VMEM((256, GRADS), bf16),
    pltpu.VMEM((2, 3, 64, FLOW_COLS), bf16),
    pltpu.VMEM((2, 64, FLOW_COLS), bf16),
    pltpu.VMEM((2, 3, 16, FLOW_COLS), bf16),
    pltpu.VMEM((2, 16, FLOW_COLS), bf16),
    pltpu.VMEM((2, 7, 16, LANES), bf16),
    pltpu.VMEM((14, 8, LANES), f32),
    pltpu.VMEM((4, 8, LANES), f32),
    pltpu.SemaphoreType.DMA((2, 4)),
    pltpu.SemaphoreType.DMA((2, 6)),
    pltpu.SemaphoreType.DMA((2, 6)),
    pltpu.SemaphoreType.DMA((2, 14)),
    pltpu.SemaphoreType.DMA((2, 14)),
    pltpu.SemaphoreType.DMA((2, 14)),
    pltpu.SemaphoreType.DMA((2, 6)),
    pltpu.SemaphoreType.DMA((2, 6)),
    pltpu.SemaphoreType.DMA((2, 8)),
]


def multiple(value, of):
    return pl.multiple_of(value, of)


class Sums:
    def __init__(self, total, out, gain_in, gain_out, scratch):
        self.total, self.out, self.gain_in, self.gain_out = total, out, gain_in, gain_out
        (self.r0, self.b1, self.r1, self.b2, self.r2, self.b3, self.r3, self.gr, self.gs) = scratch[:9]
        sems = [(s.at[0], s.at[1]) for s in scratch[9:]]
        (self.s0, self.s1, self.s2, self.s3, self.sg, self.t3, self.t2, self.t1, self.t0) = sems
        self.x, self.y, self.z, self.core = place()
        self.at = {"x": self.x, "y": self.y, "z": self.z}
        self.started = []

    def go(self, copy):
        copy.start()
        self.started.append(copy)
        return copy

    def core_send(self, n):
        cols = slice(CH * n, CH * (n + 1))
        theirs = pl.ds(multiple((1 - self.core) * 256, 256), 256)
        return self.go(
            send(self.total.at[theirs, cols], self.r0.at[:, cols], self.s0, n, along("core", 0))
        )

    def core_add(self, n):
        cols = slice(CH * n, CH * (n + 1))

        def step(i, _):
            here = pl.ds(multiple(i * 64, 64), 64)
            mine = pl.ds(multiple(self.core * 256 + i * 64, 64), 64)
            self.b1[here, cols] = (
                self.total[mine, cols].astype(f32) + self.r0[here, cols].astype(f32)
            ).astype(bf16)
            return 0

        lax.fori_loop(0, 4, step, 0)

    def first_send(self, f):
        d = FLOWS[f][0]
        cols = slice(FLOW_COLS * f, FLOW_COLS * (f + 1))
        copies = []
        for k in (1, 2, 3):
            theirs = pl.ds(multiple((self.at[d] + k) % 4 * 64, 64), 64)
            copies.append(
                self.go(send(self.b1.at[theirs, cols], self.r1.at[f, k - 1], self.s1, 3 * f + k - 1, along(d, k)))
            )
        return copies

    def first_add(self, f):
        d = FLOWS[f][0]
        cols = slice(FLOW_COLS * f, FLOW_COLS * (f + 1))

        def step(i, _):
            here = pl.ds(multiple(i * 16, 16), 16)
            mine = pl.ds(multiple(self.at[d] * 64 + i * 16, 16), 16)
            total = self.b1[mine, cols].astype(f32)
            for k in range(3):
                total += self.r1[f, k, here].astype(f32)
            self.b2[f, here] = total.astype(bf16)
            return 0

        lax.fori_loop(0, 4, step, 0)

    def second_send(self, f):
        d = FLOWS[f][1]
        copies = []
        for k in (1, 2, 3):
            theirs = pl.ds(multiple((self.at[d] + k) % 4 * 16, 16), 16)
            copies.append(
                self.go(send(self.b2.at[f, theirs], self.r2.at[f, k - 1], self.s2, 3 * f + k - 1, along(d, k)))
            )
        return copies

    def second_add(self, f):
        d = FLOWS[f][1]
        mine = pl.ds(multiple(self.at[d] * 16, 16), 16)
        total = self.b2[f, mine].astype(f32)
        for k in range(3):
            total += self.r2[f, k].astype(f32)
        self.b3[f] = total.astype(bf16)

    def third_send(self, f):
        copies = []
        for k in range(1, 8):
            theirs = pl.ds(multiple((self.z + k) % 8 * LANES, LANES), LANES)
            copies.append(
                self.go(send(self.b3.at[f, :, theirs], self.r3.at[f, k - 1], self.s3, 7 * f + k - 1, along("z", k)))
            )
        return copies

    def rows(self, f, depth):
        start = self.core * 256
        if depth >= 1:
            start = start + self.at[FLOWS[f][0]] * 64
        if depth >= 2:
            start = start + self.at[FLOWS[f][1]] * 16
        size = (256, 64, 16)[depth]
        return pl.ds(multiple(start, size), size)

    def cols(self, f):
        return pl.ds(multiple(FLOW_COLS * f + self.z * LANES, LANES), LANES)

    def third_add(self, f):
        mine = pl.ds(multiple(self.z * LANES, LANES), LANES)
        total = self.b3[f, :, mine].astype(f32)
        for k in range(7):
            total += self.r3[f, k].astype(f32)
        self.out[self.rows(f, 2), self.cols(f)] = total.astype(bf16)

    def spread_third(self, f):
        here = self.out.at[self.rows(f, 2), self.cols(f)]
        return [self.go(send(here, here, self.t3, 7 * f + k - 1, along("z", k))) for k in range(1, 8)]

    def spread_second(self, f):
        here = self.out.at[self.rows(f, 2), FLOW_COLS * f : FLOW_COLS * (f + 1)]
        return [self.go(send(here, here, self.t2, 3 * f + k - 1, along(FLOWS[f][1], k))) for k in (1, 2, 3)]

    def spread_first(self, f):
        here = self.out.at[self.rows(f, 1), FLOW_COLS * f : FLOW_COLS * (f + 1)]
        return [self.go(send(here, here, self.t1, 3 * f + k - 1, along(FLOWS[f][0], k))) for k in (1, 2, 3)]

    def spread_core(self, f, k):
        start = self.core * 256 + (self.at[FLOWS[f][0]] + 4 - k) % 4 * 64
        here = self.out.at[pl.ds(multiple(start, 64), 64), FLOW_COLS * f : FLOW_COLS * (f + 1)]
        return self.go(send(here, here, self.t0, 4 * f + k, along("core", 0)))

    def gain_send(self, stage):
        dim, slots = (("core", (0,)), ("x", (1, 2, 3)), ("y", (4, 5, 6)), ("z", tuple(range(7, 14))))[stage]
        src = self.gain_in if stage == 0 else self.gs.at[stage - 1]
        return [
            self.go(send(src, self.gr.at[slot], self.sg, slot, along(dim, i + 1)))
            for i, slot in enumerate(slots)
        ]

    def gain_add(self, stage, copies):
        slots = ((0,), (1, 2, 3), (4, 5, 6), tuple(range(7, 14)))[stage]
        total = self.gain_in[...] if stage == 0 else self.gs[stage - 1]
        for slot, copy in zip(slots, copies):
            copy.wait_recv()
            total = total + self.gr[slot]
        if stage == 3:
            self.gain_out[...] = total
        else:
            self.gs[stage] = total

    def after_core(self, core_copies, gain_copies):
        first, second, third, spread = {}, {}, {}, {}
        for f in range(2):
            for n in (2 * f, 2 * f + 1):
                core_copies[n].wait_recv()
                self.core_add(n)
            first[f] = self.first_send(f)
        self.gain_add(0, gain_copies)
        gain_copies = self.gain_send(1)
        for f in range(2):
            for copy in first[f]:
                copy.wait_recv()
            self.first_add(f)
            second[f] = self.second_send(f)
        self.gain_add(1, gain_copies)
        gain_copies = self.gain_send(2)
        for f in range(2):
            for copy in second[f]:
                copy.wait_recv()
            self.second_add(f)
            third[f] = self.third_send(f)
        self.gain_add(2, gain_copies)
        gain_copies = self.gain_send(3)
        for f in range(2):
            for copy in third[f]:
                copy.wait_recv()
            self.third_add(f)
            spread[f] = self.spread_third(f)
        self.gain_add(3, gain_copies)
        for f in range(2):
            for copy in spread[f]:
                copy.wait_recv()
            spread[f] = self.spread_second(f)
        for f in range(2):
            for copy in spread[f]:
                copy.wait_recv()
            spread[f] = self.spread_first(f)
        last = []
        for f in range(2):
            last.append(self.spread_core(f, 0))
        for k in range(3):
            for f in range(2):
                spread[f][k].wait_recv()
                last.append(self.spread_core(f, k + 1))
        return last

    def finish(self, last):
        for copy in last:
            copy.wait_recv()
        for copy in self.started:
            copy.wait_send()


ROUTES = ((0, 0, 1, 0), (0, 1, 1, 0), (0, 2, 1, 0), (0, 3, 1, 1), (1, 3, 0, 1))


def halo_neighbours():
    return [neighbour(s * a, s * b) for s in (1, -1) for a, b in ((1, 0), (0, 1), (1, 1))]


def in_kernel(tokens, cotangent, work, packed, sems):
    greet(halo_neighbours())
    copies = []
    for h in range(2):
        pack_half(h, tokens, cotangent, packed)
        for n, (hh, kind, a, b) in enumerate(ROUTES):
            if hh == h:
                copies.append(
                    send(packed.at[h, kind], work.at[h, kind], (sems.at[0], sems.at[1]), n, neighbour(-a, -b))
                )
                copies[-1].start()
    for kind in range(3):
        work[1, kind] = packed[1, kind]
    for copy in copies:
        copy.wait()


def out_kernel(
    result, total, gain_in, tokens, cotangent, layer_out, grad_tokens, out, gain_out, back, sems, *scratch
):
    greet(halo_neighbours() + partners())
    sums = Sums(total, out, gain_in, gain_out, scratch)
    core_copies = [sums.core_send(n) for n in range(4)]
    gain_copies = sums.gain_send(0)
    copies = []
    for n, (h, kind, a, b) in enumerate(ROUTES):
        copies.append(
            send(result.at[h, kind], back.at[n], (sems.at[0], sems.at[1]), n, neighbour(a, b))
        )
        copies[-1].start()
    last = sums.after_core(core_copies, gain_copies)
    for copy in copies:
        copy.wait_recv()
    unpack_half(0, [back.at[n] for n in range(4)], tokens, cotangent, layer_out, grad_tokens)
    unpack_half(
        1,
        [result.at[1, kind] for kind in range(3)] + [back.at[4]],
        tokens,
        cotangent,
        layer_out,
        grad_tokens,
    )
    sums.finish(last)
    for copy in copies:
        copy.wait_send()


VMEM = pl.BlockSpec(memory_space=pltpu.VMEM)
LIMIT = 56 * 1024 * 1024


def local(tokens, cotangent, w_qkv, w_out, norm_gain_vector):
    gain = norm_gain_vector.reshape(1, CH)
    shape = jax.ShapeDtypeStruct
    work = pl.pallas_call(
        in_kernel,
        out_shape=shape((2, 4, CHUNK, CH), bf16),
        in_specs=[VMEM] * 2,
        out_specs=VMEM,
        scratch_shapes=[pltpu.VMEM((2, 4, CHUNK, CH), bf16), pltpu.SemaphoreType.DMA((2, 5))],
        compiler_params=pltpu.CompilerParams(
            collective_id=0, has_side_effects=True, vmem_limit_bytes=LIMIT
        ),
    )(tokens, cotangent)
    result, total, gain_in = pl.pallas_call(
        compute_kernel,
        out_shape=(
            shape((2, 4, CHUNK, CH), bf16),
            shape((CH, GRADS), bf16),
            shape((8, LANES), f32),
        ),
        in_specs=[VMEM] * 4,
        out_specs=(VMEM,) * 3,
        scratch_shapes=WINDOW_SCRATCH,
        compiler_params=pltpu.CompilerParams(vmem_limit_bytes=LIMIT),
    )(work, w_qkv, w_out, gain)
    layer_out, grad_tokens, out, gain_out = pl.pallas_call(
        out_kernel,
        out_shape=(
            shape(tokens.shape, bf16),
            shape(tokens.shape, bf16),
            shape((CH, GRADS), bf16),
            shape((8, LANES), f32),
        ),
        in_specs=[VMEM] * 5,
        out_specs=(VMEM,) * 4,
        scratch_shapes=[pltpu.VMEM((5, CHUNK, CH), bf16), pltpu.SemaphoreType.DMA((2, 5))]
        + SUM_SCRATCH,
        compiler_params=pltpu.CompilerParams(
            collective_id=1, has_side_effects=True, vmem_limit_bytes=LIMIT
        ),
    )(result, total, gain_in, tokens, cotangent)
    return (
        layer_out,
        grad_tokens,
        out[:, : 3 * CH],
        out[:, 3 * CH :],
        gain_out[:4].reshape(CH),
    )


def solution(mesh):
    return jax.shard_map(
        local,
        mesh=mesh,
        in_specs=(P(None, "lat", "lon", None), P(None, "lat", "lon", None), P(), P(), P()),
        out_specs=(P(None, "lat", "lon", None), P(None, "lat", "lon", None), P(), P(), P()),
        check_vma=False,
    )
```

```python
import functools

import jax
import jax.numpy as jnp
from jax import lax
from jax.experimental import pallas as pl
from jax.experimental.pallas import tpu as pltpu
from jax.sharding import PartitionSpec as P

CH = 512
HEADS = 8
HEAD_DIM = CH // HEADS
LEVELS = 4
ROWS = 6
HALF = 3
COLS = 24
SPAN = 144
CHUNK = 144
LAST_BAND = 7
GRADS = 4 * CH
SCALE = HEAD_DIM ** (-0.5)
LOG2E = 1.4426950408889634
MASKED = -1e30
LANES = 128
MESH = pl.DeviceIdType.MESH
f32 = jnp.float32
bf16 = jnp.bfloat16


def nt(a, b):
    return lax.dot_general(a, b, (((1,), (1,)), ((), ())), preferred_element_type=f32)


def tn(a, b):
    return lax.dot_general(a, b, (((0,), (0,)), ((), ())), preferred_element_type=f32)


def nn(a, b):
    return lax.dot_general(a, b, (((1,), (0,)), ((), ())), preferred_element_type=f32)


def turned(v, by):
    by = by % COLS
    return v if by == 0 else pltpu.roll(v, by, axis=0)


def place():
    lat, lon = lax.axis_index("lat"), lax.axis_index("lon")
    y, x_hi = lat // 2, lat % 2
    x_lo, z, core = lon // 16, (lon % 16) // 2, lon % 2
    return 2 * x_hi + x_lo, y, z, core


def device_at(x, y, z, core):
    return (2 * y + x // 2, 16 * (x % 2) + 2 * z + core)


def neighbour(by_lat, by_lon):
    lat, lon = lax.axis_index("lat"), lax.axis_index("lon")
    return ((lat + by_lat + 8) % 8, (lon + by_lon + 32) % 32)


def along(dim, k):
    x, y, z, core = place()
    if dim == "x":
        return device_at((x + k) % 4, y, z, core)
    if dim == "y":
        return device_at(x, (y + k) % 4, z, core)
    if dim == "z":
        return device_at(x, y, (z + k) % 8, core)
    return device_at(x, y, z, 1 - core)


def send(src, dst, sems, slot, device):
    return pltpu.make_async_remote_copy(
        src_ref=src,
        dst_ref=dst,
        send_sem=sems[0].at[slot],
        recv_sem=sems[1].at[slot],
        device_id=device,
        device_id_type=MESH,
    )


def greet(devices):
    for device in devices:
        pl.semaphore_signal(
            pltpu.get_barrier_semaphore(), inc=1, device_id=device, device_id_type=MESH
        )


def pack_half(h, first, second, packed):
    row = lax.broadcasted_iota(jnp.int32, (COLS, LANES), 0)

    def lanes_step(c, _):
        lanes = pl.ds(pl.multiple_of(c * LANES, LANES), LANES)
        kinds = [[], [], [], []]
        for src in (first, second):
            for i in range(HALF):
                v0, v1, v2, v3 = (
                    src[l, HALF * h + i, :, lanes].astype(f32) for l in range(LEVELS)
                )
                kinds[0].append(jnp.where(row < 12, turned(v1, -6), turned(v2, 6)))
                kinds[1].append(jnp.where(row < 12, turned(v3, -6), turned(v0, 6)))
                kinds[2].append(
                    jnp.where(
                        row < 12,
                        jnp.where(row < 6, turned(v1, 6), turned(v2, 12)),
                        jnp.where(row < 18, turned(v3, 18), v0),
                    )
                )
                kinds[3].append(
                    jnp.where(
                        row < 12,
                        jnp.where(row < 6, v1, turned(v2, 6)),
                        jnp.where(row < 18, turned(v3, 12), turned(v0, 18)),
                    )
                )
        for kind in range(4):
            packed[h, kind, :, lanes] = jnp.concatenate(kinds[kind], axis=0).astype(bf16)
        return 0

    lax.fori_loop(0, CH // LANES, lanes_step, 0)


def unpack_half(h, chunks, first, second, first_out, second_out):
    row = lax.broadcasted_iota(jnp.int32, (COLS, LANES), 0)

    def lanes_step(c, _):
        lanes = pl.ds(pl.multiple_of(c * LANES, LANES), LANES)
        kinds = [chunks[kind][:, lanes].astype(f32) for kind in range(4)]
        for n, (src, out) in enumerate(((first, first_out), (second, second_out))):
            for i in range(HALF):
                at = 72 * n + COLS * i
                a0, a1, b, e = (kind[at : at + COLS] for kind in kinds)
                west, east = row < 6, row >= 18
                v1 = jnp.where(west, e, jnp.where(east, turned(b, 18), turned(a0, 6)))
                v2 = jnp.where(
                    west, turned(e, 18), jnp.where(east, turned(b, 12), turned(a0, 18))
                )
                v3 = jnp.where(
                    west, turned(e, 12), jnp.where(east, turned(b, 6), turned(a1, 6))
                )
                v0 = jnp.where(west, turned(e, 6), jnp.where(east, b, turned(a1, 18)))
                for l, v in enumerate((v0, v1, v2, v3)):
                    r = HALF * h + i
                    total = src[l, r, :, lanes].astype(f32) + v
                    out[l, r, :, lanes] = total.astype(bf16)
        return 0

    lax.fori_loop(0, CH // LANES, lanes_step, 0)


def by_pair(blocks):
    row = lax.broadcasted_iota(jnp.int32, blocks[0].shape, 0)
    pairs = ([], [])
    for j in range(3):
        a, b = blocks[2 * j], blocks[2 * j + 1]
        pairs[0].append(jnp.where(row < 12, a, turned(b, 12)))
        pairs[1].append(jnp.where(row < 12, turned(a, 12), b))
    return pairs


def by_row(pairs):
    row = lax.broadcasted_iota(jnp.int32, pairs[0][0].shape, 0)
    blocks = []
    for j in range(3):
        a, b = pairs[0][j], pairs[1][j]
        blocks.append(jnp.where(row < 12, a, turned(b, 12)))
        blocks.append(jnp.where(row < 12, turned(a, 12), b))
    return blocks


def blocks_of(value, n):
    return [value[72 * n + COLS * i : 72 * n + COLS * (i + 1)] for i in range(HALF)]


def set_bias(bias):
    last = (lax.axis_index("lat") == LAST_BAND).astype(jnp.int32)
    shape = (SPAN, SPAN)
    for s in range(2):
        labels = []
        for dim in range(2):
            i = lax.broadcasted_iota(jnp.int32, shape, dim)
            if s == 0:
                lat_row = i // COLS
                level = (i % COLS) // 12
            else:
                t = i % 72
                u = t % COLS
                lat_row = 2 * (t // COLS) + u // 12
                level = (u % 12) // 6
            labels.append((last * (lat_row < HALF).astype(jnp.int32), level))
        (kr, kl), (qr, ql) = labels
        same_row = kr == qr
        bias[s, 0] = jnp.where(same_row, 0.0, MASKED).astype(f32)
        bias[s, 1] = jnp.where(same_row & (kl == ql), 0.0, MASKED).astype(f32)


def norm_block(x, gain):
    mean = jnp.mean(x, axis=-1, keepdims=True)
    centered = x - mean
    inverse = lax.rsqrt(jnp.mean(centered * centered, axis=-1, keepdims=True) + 1e-05)
    xhat = centered * inverse
    return xhat, inverse, (xhat * gain).astype(bf16)


def load_windows(s, chunk_ref, gain_ref, normed, grads, xhat_ref, inverse_ref):
    gain = gain_ref[...]
    base = 2 * SPAN * s

    def store(off, xs, gs):
        x = jnp.concatenate(xs, axis=0)
        xhat, inverse, n = norm_block(x, gain)
        xhat_ref[base + off : base + off + 48] = xhat
        inverse_ref[base + off : base + off + 48] = jnp.broadcast_to(inverse, (48, LANES))
        normed[base + off : base + off + 48] = n
        grads[base + off : base + off + 48] = jnp.concatenate(gs, axis=0).astype(bf16)

    if s == 0:
        for p in range(2):
            halves = [chunk_ref(h, p)[...].astype(f32) for h in range(2)]
            xs = sum((blocks_of(v, 0) for v in halves), [])
            gs = sum((blocks_of(v, 1) for v in halves), [])
            for j in range(3):
                store(SPAN * p + 48 * j, xs[2 * j : 2 * j + 2], gs[2 * j : 2 * j + 2])
    else:
        parts = []
        for n in range(2):
            sides = []
            for kind in (2, 3):
                halves = [chunk_ref(h, kind)[...].astype(f32) for h in range(2)]
                sides.append(by_pair(sum((blocks_of(v, n) for v in halves), [])))
            parts.append([sides[0][p] + sides[1][p] for p in range(2)])
        for p in range(2):
            for j in range(3):
                store(
                    SPAN * p + 48 * j,
                    parts[0][p][2 * j : 2 * j + 2],
                    parts[1][p][2 * j : 2 * j + 2],
                )


def head_pair(s, p, lanes_of, bias, qkv, d_attn, attn, d_qkv):
    rows = slice(SPAN * p, SPAN * (p + 1))
    base = 2 * SPAN * s + SPAN * p
    out_rows = slice(base, base + SPAN)
    q = qkv[rows, lanes_of(0)]
    k = qkv[rows, lanes_of(1)]
    v = qkv[rows, lanes_of(2)]
    g = d_attn[rows, lanes_of(0)]
    lane = lax.broadcasted_iota(jnp.int32, (SPAN, LANES), 1)
    o, dq, dk, dv = [], [], [], []
    for e in range(2):
        mine = (lane < HEAD_DIM) if e == 0 else (lane >= HEAD_DIM)
        zero = jnp.zeros((), bf16)
        qm = jnp.where(mine, q, zero)
        km = jnp.where(mine, k, zero)
        vm = jnp.where(mine, v, zero)
        gm = jnp.where(mine, g, zero)
        scores = nt(k, qm) * (SCALE * LOG2E) + bias[s, p]
        top = jnp.max(scores, axis=0, keepdims=True)
        expo = jnp.exp2(scores - top)
        probs = expo * (1.0 / jnp.sum(expo, axis=0, keepdims=True))
        probs_b = probs.astype(bf16)
        d_probs = nt(v, gm)
        mean = jnp.sum(d_probs * probs, axis=0, keepdims=True)
        d_scores = (probs * (d_probs - mean) * SCALE).astype(bf16)
        o.append(tn(probs_b, vm))
        dv.append(nn(probs_b, gm))
        dq.append(tn(d_scores, km))
        dk.append(nn(d_scores, qm))
    attn[out_rows, lanes_of(0)] = (o[0] + o[1]).astype(bf16)
    d_qkv[out_rows, lanes_of(0)] = (dq[0] + dq[1]).astype(bf16)
    d_qkv[out_rows, lanes_of(1)] = (dk[0] + dk[1]).astype(bf16)
    d_qkv[out_rows, lanes_of(2)] = (dv[0] + dv[1]).astype(bf16)


def windows_front(s, chunk_ref, w, scratch):
    w_qkv, w_out, gain_ref = w
    (normed, grads, attn, d_qkv, qkv, d_attn, xhat_ref, inverse_ref, branch, shifted, bias, gain_sum) = scratch
    base = 2 * SPAN * s
    rows = slice(base, base + 2 * SPAN)
    load_windows(s, chunk_ref, gain_ref, normed, grads, xhat_ref, inverse_ref)
    for n in range(3):
        cols = slice(CH * n, CH * (n + 1))
        qkv[:, cols] = nn(normed[rows], w_qkv[:, cols]).astype(bf16)
    d_attn[...] = nt(grads[rows], w_out[...]).astype(bf16)

    def pair_step(hp, _):
        def lanes_of(n):
            return pl.ds(pl.multiple_of(CH * n + LANES * hp, LANES), LANES)

        for p in range(2):
            head_pair(s, p, lanes_of, bias, qkv, d_attn, attn, d_qkv)
        return 0

    lax.fori_loop(0, HEADS // 2, pair_step, 0)


def windows_back(s, result_ref, w, scratch):
    w_qkv, w_out, gain_ref = w
    (normed, grads, attn, d_qkv, qkv, d_attn, xhat_ref, inverse_ref, branch, shifted, bias, gain_sum) = scratch
    base = 2 * SPAN * s
    rows = slice(base, base + 2 * SPAN)
    branch[...] = nn(attn[rows], w_out[...])
    shifted[...] = nt(d_qkv[rows], w_qkv[...])
    gain = gain_ref[...]
    for i in range(6):
        at = slice(48 * i, 48 * (i + 1))
        there = slice(base + 48 * i, base + 48 * (i + 1))
        d_normed = shifted[at]
        xhat = xhat_ref[there]
        gain_sum[...] += jnp.sum((d_normed * xhat).reshape(6, 8, CH), axis=0)
        d_xhat = d_normed * gain
        mean = jnp.mean(d_xhat, axis=-1, keepdims=True)
        slope = jnp.mean(d_xhat * xhat, axis=-1, keepdims=True)
        shifted[at] = inverse_ref[there, 0:1] * (d_xhat - mean - xhat * slope)
    if s == 0:
        for p in range(2):
            for h in range(2):
                at = slice(SPAN * p + 72 * h, SPAN * p + 72 * (h + 1))
                result_ref(h, p)[...] = jnp.concatenate(
                    [branch[at], shifted[at]], axis=0
                ).astype(bf16)
    else:
        for side, kind in enumerate((2, 3)):
            blocks = []
            for value in (branch, shifted):
                pairs = [
                    [
                        value[SPAN * p + 72 * side + COLS * j : SPAN * p + 72 * side + COLS * (j + 1)]
                        for j in range(3)
                    ]
                    for p in range(2)
                ]
                blocks.append(by_row(pairs))
            for h in range(2):
                result_ref(h, kind)[...] = jnp.concatenate(
                    blocks[0][HALF * h : HALF * h + HALF] + blocks[1][HALF * h : HALF * h + HALF],
                    axis=0,
                ).astype(bf16)


def weight_grads(n, total, scratch):
    normed, grads, attn, d_qkv = scratch[:4]
    cols = slice(CH * n, CH * (n + 1))
    if n < 3:
        total[:, cols] = tn(normed[...], d_qkv[:, cols]).astype(bf16)
    else:
        total[:, cols] = tn(attn[...], grads[...]).astype(bf16)


def gain_rows(gain_sum, gain_out):
    row = jnp.sum(gain_sum[...], axis=0, keepdims=True)
    gain_out[...] = jnp.concatenate(
        [row[:, LANES * i : LANES * (i + 1)] for i in range(4)] + [jnp.zeros((4, LANES), f32)],
        axis=0,
    )


WINDOW_SCRATCH = [
    pltpu.VMEM((4 * SPAN, CH), bf16),
    pltpu.VMEM((4 * SPAN, CH), bf16),
    pltpu.VMEM((4 * SPAN, CH), bf16),
    pltpu.VMEM((4 * SPAN, 3 * CH), bf16),
    pltpu.VMEM((2 * SPAN, 3 * CH), bf16),
    pltpu.VMEM((2 * SPAN, CH), bf16),
    pltpu.VMEM((4 * SPAN, CH), f32),
    pltpu.VMEM((4 * SPAN, LANES), f32),
    pltpu.VMEM((2 * SPAN, CH), f32),
    pltpu.VMEM((2 * SPAN, CH), f32),
    pltpu.VMEM((2, 2, SPAN, SPAN), f32),
    pltpu.VMEM((8, CH), f32),
]


ORDER = (3, 0, 1, 2)
DIMS = (("x", "y"), ("y", "x"), ("x", "y"), ("y", "x"))


def partners():
    return (
        [along("core", 0)]
        + [along("x", k) for k in (1, 2, 3)]
        + [along("y", k) for k in (1, 2, 3)]
        + [along("z", k) for k in range(1, 8)]
    )


SUM_SCRATCH = [
    pltpu.VMEM((CH, GRADS), bf16),
    pltpu.VMEM((CH, GRADS), bf16),
    pltpu.VMEM((8, LANES), f32),
    pltpu.VMEM((256, GRADS), bf16),
    pltpu.VMEM((256, GRADS), bf16),
    pltpu.VMEM((4, 3, 64, CH), bf16),
    pltpu.VMEM((4, 64, CH), bf16),
    pltpu.VMEM((4, 3, 16, CH), bf16),
    pltpu.VMEM((2, 8, 16, 2 * CH), bf16),
    pltpu.VMEM((4, 8, 8, LANES), f32),
    pltpu.SemaphoreType.DMA((2, 4)),
    pltpu.SemaphoreType.DMA((2, 12)),
    pltpu.SemaphoreType.DMA((2, 12)),
    pltpu.SemaphoreType.DMA((2, 14)),
    pltpu.SemaphoreType.DMA((2, 14)),
    pltpu.SemaphoreType.DMA((2, 12)),
    pltpu.SemaphoreType.DMA((2, 12)),
    pltpu.SemaphoreType.DMA((2, 4)),
]


def ds(start, size):
    return pl.ds(pl.multiple_of(start, size), size)


class Sums:
    def __init__(self, gain_out, scratch):
        (self.total, self.out, self.gain_in, self.r0, self.b1, self.r1, self.b2, self.r2, self.zs, self.gs) = scratch[:10]
        sems = [(s.at[0], s.at[1]) for s in scratch[10:]]
        (self.s0, self.s1, self.s2, self.s3, self.sg, self.t2, self.t1, self.t0) = sems
        self.gain_out = gain_out
        x, y, z, core = place()
        self.at = {"x": x, "y": y, "z": z, "core": core}
        self.core = core
        self.started = []

    def go(self, copy):
        copy.start()
        self.started.append(copy)
        return copy

    def cols(self, j):
        n = ORDER[j]
        return slice(CH * n, CH * (n + 1))

    def core_send(self, j):
        cols = self.cols(j)
        theirs = ds((1 - self.core) * 256, 256)
        return self.go(
            send(self.total.at[theirs, cols], self.r0.at[:, cols], self.s0, j, along("core", 0))
        )

    def core_add(self, j):
        cols = self.cols(j)

        def step(i, _):
            here = ds(i * 64, 64)
            mine = ds(self.core * 256 + i * 64, 64)
            self.b1[here, cols] = (
                self.total[mine, cols].astype(f32) + self.r0[here, cols].astype(f32)
            ).astype(bf16)
            return 0

        lax.fori_loop(0, 4, step, 0)

    def first_send(self, j):
        d = DIMS[j][0]
        return [
            self.go(
                send(
                    self.b1.at[ds((self.at[d] + k) % 4 * 64, 64), self.cols(j)],
                    self.r1.at[j, k - 1],
                    self.s1,
                    3 * j + k - 1,
                    along(d, k),
                )
            )
            for k in (2, 1, 3)
        ]

    def first_add(self, j):
        d = DIMS[j][0]

        def step(i, _):
            here = ds(i * 16, 16)
            mine = ds(self.at[d] * 64 + i * 16, 16)
            total = self.b1[mine, self.cols(j)].astype(f32)
            for k in range(3):
                total += self.r1[j, k, here].astype(f32)
            self.b2[j, here] = total.astype(bf16)
            return 0

        lax.fori_loop(0, 4, step, 0)

    def second_send(self, j):
        d = DIMS[j][1]
        return [
            self.go(
                send(
                    self.b2.at[j, ds((self.at[d] + k) % 4 * 16, 16)],
                    self.r2.at[j, k - 1],
                    self.s2,
                    3 * j + k - 1,
                    along(d, k),
                )
            )
            for k in (2, 1, 3)
        ]

    def second_add(self, j):
        mine = ds(self.at[DIMS[j][1]] * 16, 16)
        total = self.b2[j, mine].astype(f32)
        for k in range(3):
            total += self.r2[j, k].astype(f32)
        cols = slice(CH * (j % 2), CH * (j % 2 + 1))
        self.zs[j // 2, self.at["z"], :, cols] = total.astype(bf16)

    def third_send(self, g):
        here = self.zs.at[g, self.at["z"]]
        return [
            self.go(send(here, here, self.s3, 7 * g + k - 1, along("z", k)))
            for k in (4, 3, 5, 2, 6, 1, 7)
        ]

    def rows(self, j, depth):
        start = self.core * 256
        if depth >= 1:
            start = start + self.at[DIMS[j][0]] * 64
        if depth >= 2:
            start = start + self.at[DIMS[j][1]] * 16
        return ds(start, (256, 64, 16)[depth])

    def third_add(self, g):
        total = self.zs[g, 0].astype(f32)
        for z in range(1, 8):
            total += self.zs[g, z].astype(f32)
        total = total.astype(bf16)
        for i in range(2):
            j = 2 * g + i
            self.out[self.rows(j, 2), self.cols(j)] = total[:, CH * i : CH * (i + 1)]

    def spread(self, j, depth):
        here = self.out.at[self.rows(j, depth), self.cols(j)]
        if depth == 0:
            return [self.go(send(here, here, self.t0, j, along("core", 0)))]
        d, sems = DIMS[j][depth - 1], (self.t1, self.t2)[depth - 1]
        return [self.go(send(here, here, sems, 3 * j + k - 1, along(d, k))) for k in (2, 1, 3)]

    def gain_send(self, stage):
        dim, size, first = (("core", 2, 0), ("x", 4, 1), ("y", 4, 4), ("z", 8, 7))[stage]
        here = self.gs.at[stage, self.at[dim]]
        return [
            self.go(send(here, here, self.sg, first + k - 1, along(dim, k)))
            for k in range(1, size)
        ]

    def gain_add(self, stage, copies):
        for copy in copies:
            copy.wait_recv()
        total = self.gs[stage, 0]
        for i in range(1, (2, 4, 4, 8)[stage]):
            total = total + self.gs[stage, i]
        if stage == 3:
            self.gain_out[...] = total
        else:
            self.gs[stage + 1, self.at["xyz"[stage]]] = total


def arrived(copies):
    for copy in copies:
        copy.wait_recv()


ROUTES = ((0, 0, 1, 0), (0, 1, 1, 0), (0, 2, 1, 0), (0, 3, 1, 1), (1, 3, 0, 1))


def halo_neighbours():
    return [neighbour(s * a, s * b) for s in (1, -1) for a, b in ((1, 0), (0, 1), (1, 1))]


def layer_kernel(
    tokens_hbm, cotangent_hbm, w_qkv_hbm, w_out_hbm, gain,
    layer_out, grad_tokens, grad_qkv, grad_out, gain_out,
    packed, work, result, back, tokens, cotangent, layer_buf, grad_buf, w_qkv, w_out,
    in_sems, out_sems, copy_sems, *scratch,
):
    window_scratch, sum_scratch = scratch[: len(WINDOW_SCRATCH)], scratch[len(WINDOW_SCRATCH) :]
    tokens_in = []
    for h in range(2):
        rows = slice(HALF * h, HALF * (h + 1))
        for n, (src, dst) in enumerate(((tokens_hbm, tokens), (cotangent_hbm, cotangent))):
            tokens_in.append(
                pltpu.make_async_copy(src.at[:, rows], dst.at[:, rows], copy_sems.at[8 + 2 * h + n])
            )
            tokens_in[-1].start()
    weights_in = [
        pltpu.make_async_copy(w_qkv_hbm, w_qkv, copy_sems.at[0]),
        pltpu.make_async_copy(w_out_hbm, w_out, copy_sems.at[1]),
    ]
    for copy in weights_in:
        copy.start()
    greeted = halo_neighbours() + partners()
    greet(greeted)
    for copy in tokens_in[:2]:
        copy.wait()
    pack_half(0, tokens, cotangent, packed)
    pl.semaphore_wait(pltpu.get_barrier_semaphore(), len(greeted))
    inward = []
    for n, (h, kind, a, b) in enumerate(ROUTES):
        if n == 4:
            for copy in tokens_in[2:]:
                copy.wait()
            pack_half(1, tokens, cotangent, packed)
        copy = send(
            packed.at[h, kind], work.at[n], (in_sems.at[0], in_sems.at[1]), n, neighbour(-a, -b)
        )
        copy.start()
        inward.append(copy)

    def chunk_ref(h, kind):
        if h == 1 and kind < 3:
            return packed.at[1, kind]
        return work.at[4 if h == 1 else kind]

    sums = Sums(gain_out, sum_scratch)
    set_bias(window_scratch[10])
    window_scratch[11][...] = jnp.zeros((8, CH), f32)
    w = (w_qkv, w_out, gain)
    for copy in weights_in:
        copy.wait()
    arrived(inward[0:2])
    windows_front(0, chunk_ref, w, window_scratch)
    arrived(inward[2:5])
    windows_front(1, chunk_ref, w, window_scratch)

    by_core, first, second, third, spread2, spread1, spread0 = {}, {}, {}, {}, {}, {}, {}
    for j in range(4):
        weight_grads(ORDER[j], sums.total, window_scratch)
        by_core[j] = sums.core_send(j)
        if j >= 1:
            by_core[j - 1].wait_recv()
            sums.core_add(j - 1)
            first[j - 1] = sums.first_send(j - 1)
    by_core[3].wait_recv()
    sums.core_add(3)
    first[3] = sums.first_send(3)

    for s in range(2):
        windows_back(s, lambda h, kind: result.at[h, kind], w, window_scratch)
    gain_rows(window_scratch[11], sums.gain_in)
    sums.gs[0, sums.core] = sums.gain_in[...]
    by_gain = sums.gain_send(0)
    for j in range(4):
        arrived(first[j])
        sums.first_add(j)
        second[j] = sums.second_send(j)
    outward = []
    for n, (h, kind, a, b) in enumerate(ROUTES):
        copy = send(
            result.at[h, kind], back.at[n], (out_sems.at[0], out_sems.at[1]), n, neighbour(a, b)
        )
        copy.start()
        outward.append(copy)
    sums.gain_add(0, by_gain)
    by_gain = sums.gain_send(1)
    for g in range(2):
        for j in (2 * g, 2 * g + 1):
            arrived(second[j])
            sums.second_add(j)
        third[g] = sums.third_send(g)
    sums.gain_add(1, by_gain)
    by_gain = sums.gain_send(2)
    for g in range(2):
        arrived(third[g])
        sums.third_add(g)
        for j in (2 * g, 2 * g + 1):
            spread2[j] = sums.spread(j, 2)
    sums.gain_add(2, by_gain)
    by_gain = sums.gain_send(3)

    arrived(outward)
    unpack_half(0, [back.at[n] for n in range(4)], tokens, cotangent, layer_buf, grad_buf)
    unpack_half(
        1,
        [result.at[1, kind] for kind in range(3)] + [back.at[4]],
        tokens,
        cotangent,
        layer_buf,
        grad_buf,
    )
    outputs = [
        pltpu.make_async_copy(layer_buf, layer_out, copy_sems.at[2]),
        pltpu.make_async_copy(grad_buf, grad_tokens, copy_sems.at[3]),
    ]
    for copy in outputs:
        copy.start()

    for j in range(4):
        arrived(spread2[j])
        spread1[j] = sums.spread(j, 1)
    sums.gain_add(3, by_gain)
    for j in range(4):
        arrived(spread1[j])
        spread0[j] = sums.spread(j, 0)
    for j in range(4):
        arrived(spread0[j])
        n = ORDER[j]
        cols = slice(CH * n, CH * (n + 1))
        outputs.append(
            pltpu.make_async_copy(
                sums.out.at[:, cols],
                grad_qkv.at[:, cols] if n < 3 else grad_out,
                copy_sems.at[4 + j],
            )
        )
        outputs[-1].start()
    for copy in inward + outward + sums.started:
        copy.wait_send()
    for copy in outputs:
        copy.wait()


VMEM = pl.BlockSpec(memory_space=pltpu.VMEM)
ANY = pl.BlockSpec(memory_space=pl.ANY)
LIMIT = 60 * 1024 * 1024


def local(tokens, cotangent, w_qkv, w_out, norm_gain_vector):
    shape = jax.ShapeDtypeStruct
    layer_out, grad_tokens, grad_qkv, grad_out, gain_out = pl.pallas_call(
        layer_kernel,
        out_shape=(
            shape(tokens.shape, bf16),
            shape(tokens.shape, bf16),
            shape((CH, 3 * CH), bf16),
            shape((CH, CH), bf16),
            shape((8, LANES), f32),
        ),
        in_specs=[ANY, ANY, ANY, ANY, VMEM],
        out_specs=(ANY, ANY, ANY, ANY, VMEM),
        scratch_shapes=[
            pltpu.VMEM((2, 4, CHUNK, CH), bf16),
            pltpu.VMEM((5, CHUNK, CH), bf16),
            pltpu.VMEM((2, 4, CHUNK, CH), bf16),
            pltpu.VMEM((5, CHUNK, CH), bf16),
            pltpu.VMEM(tokens.shape, bf16),
            pltpu.VMEM(tokens.shape, bf16),
            pltpu.VMEM(tokens.shape, bf16),
            pltpu.VMEM(tokens.shape, bf16),
            pltpu.VMEM((CH, 3 * CH), bf16),
            pltpu.VMEM((CH, CH), bf16),
            pltpu.SemaphoreType.DMA((2, 5)),
            pltpu.SemaphoreType.DMA((2, 5)),
            pltpu.SemaphoreType.DMA((12,)),
        ]
        + WINDOW_SCRATCH
        + SUM_SCRATCH,
        compiler_params=pltpu.CompilerParams(
            collective_id=0, has_side_effects=True, vmem_limit_bytes=LIMIT
        ),
    )(tokens, cotangent, w_qkv, w_out, norm_gain_vector.reshape(1, CH))
    return (layer_out, grad_tokens, grad_qkv, grad_out, gain_out[:4].reshape(CH))


def solution(mesh):
    return jax.shard_map(
        local,
        mesh=mesh,
        in_specs=(P(None, "lat", "lon", None), P(None, "lat", "lon", None), P(), P(), P()),
        out_specs=(P(None, "lat", "lon", None), P(None, "lat", "lon", None), P(), P(), P()),
        check_vma=False,
    )
```

```python
import functools

import jax
import jax.numpy as jnp
from jax import lax
from jax.experimental import pallas as pl
from jax.experimental.pallas import tpu as pltpu
from jax.sharding import PartitionSpec as P

CH = 512
HEADS = 8
HEAD_DIM = CH // HEADS
LEVELS = 4
ROWS = 6
HALF = 3
COLS = 24
SPAN = 144
CHUNK = 144
LAST_BAND = 7
GRADS = 4 * CH
SCALE = HEAD_DIM ** (-0.5)
LOG2E = 1.4426950408889634
MASKED = -1e30
LANES = 128
GROUP = 4
GROUP_LANES = GROUP * HEAD_DIM
MESH = pl.DeviceIdType.MESH
f32 = jnp.float32
bf16 = jnp.bfloat16


def nt(a, b):
    return lax.dot_general(a, b, (((1,), (1,)), ((), ())), preferred_element_type=f32)


def tn(a, b):
    return lax.dot_general(a, b, (((0,), (0,)), ((), ())), preferred_element_type=f32)


def nn(a, b):
    return lax.dot_general(a, b, (((1,), (0,)), ((), ())), preferred_element_type=f32)


def turned(v, by):
    by = by % COLS
    return v if by == 0 else pltpu.roll(v, by, axis=0)


def place():
    lat, lon = lax.axis_index("lat"), lax.axis_index("lon")
    y, x_hi = lat // 2, lat % 2
    x_lo, z, core = lon // 16, (lon % 16) // 2, lon % 2
    return 2 * x_hi + x_lo, y, z, core


def device_at(x, y, z, core):
    return (2 * y + x // 2, 16 * (x % 2) + 2 * z + core)


def neighbour(by_lat, by_lon):
    lat, lon = lax.axis_index("lat"), lax.axis_index("lon")
    return ((lat + by_lat + 8) % 8, (lon + by_lon + 32) % 32)


def along(dim, k):
    x, y, z, core = place()
    if dim == "x":
        return device_at((x + k) % 4, y, z, core)
    if dim == "y":
        return device_at(x, (y + k) % 4, z, core)
    if dim == "z":
        return device_at(x, y, (z + k) % 8, core)
    return device_at(x, y, z, 1 - core)


def send(src, dst, sems, slot, device):
    return pltpu.make_async_remote_copy(
        src_ref=src,
        dst_ref=dst,
        send_sem=sems[0].at[slot],
        recv_sem=sems[1].at[slot],
        device_id=device,
        device_id_type=MESH,
    )


def greet(devices):
    for device in devices:
        pl.semaphore_signal(
            pltpu.get_barrier_semaphore(), inc=1, device_id=device, device_id_type=MESH
        )


def pack_half(h, first, second, packed):
    row = lax.broadcasted_iota(jnp.int32, (COLS, LANES), 0)

    def lanes_step(c, _):
        lanes = pl.ds(pl.multiple_of(c * LANES, LANES), LANES)
        kinds = [[], [], [], []]
        for src in (first, second):
            for i in range(HALF):
                v0, v1, v2, v3 = (
                    src[l, HALF * h + i, :, lanes].astype(f32) for l in range(LEVELS)
                )
                kinds[0].append(jnp.where(row < 12, turned(v1, -6), turned(v2, 6)))
                kinds[1].append(jnp.where(row < 12, turned(v3, -6), turned(v0, 6)))
                kinds[2].append(
                    jnp.where(
                        row < 12,
                        jnp.where(row < 6, turned(v1, 6), turned(v2, 12)),
                        jnp.where(row < 18, turned(v3, 18), v0),
                    )
                )
                kinds[3].append(
                    jnp.where(
                        row < 12,
                        jnp.where(row < 6, v1, turned(v2, 6)),
                        jnp.where(row < 18, turned(v3, 12), turned(v0, 18)),
                    )
                )
        for kind in range(4):
            packed[h, kind, :, lanes] = jnp.concatenate(kinds[kind], axis=0).astype(bf16)
        return 0

    lax.fori_loop(0, CH // LANES, lanes_step, 0)


def unpack_half(h, chunks, first, second, first_out, second_out):
    row = lax.broadcasted_iota(jnp.int32, (COLS, LANES), 0)

    def lanes_step(c, _):
        lanes = pl.ds(pl.multiple_of(c * LANES, LANES), LANES)
        kinds = [chunks[kind][:, lanes].astype(f32) for kind in range(4)]
        for n, (src, out) in enumerate(((first, first_out), (second, second_out))):
            for i in range(HALF):
                at = 72 * n + COLS * i
                a0, a1, b, e = (kind[at : at + COLS] for kind in kinds)
                west, east = row < 6, row >= 18
                v1 = jnp.where(west, e, jnp.where(east, turned(b, 18), turned(a0, 6)))
                v2 = jnp.where(
                    west, turned(e, 18), jnp.where(east, turned(b, 12), turned(a0, 18))
                )
                v3 = jnp.where(
                    west, turned(e, 12), jnp.where(east, turned(b, 6), turned(a1, 6))
                )
                v0 = jnp.where(west, turned(e, 6), jnp.where(east, b, turned(a1, 18)))
                for l, v in enumerate((v0, v1, v2, v3)):
                    r = HALF * h + i
                    total = src[l, r, :, lanes].astype(f32) + v
                    out[l, r, :, lanes] = total.astype(bf16)
        return 0

    lax.fori_loop(0, CH // LANES, lanes_step, 0)


def by_pair(blocks):
    row = lax.broadcasted_iota(jnp.int32, blocks[0].shape, 0)
    pairs = ([], [])
    for j in range(3):
        a, b = blocks[2 * j], blocks[2 * j + 1]
        pairs[0].append(jnp.where(row < 12, a, turned(b, 12)))
        pairs[1].append(jnp.where(row < 12, turned(a, 12), b))
    return pairs


def by_row(pairs):
    row = lax.broadcasted_iota(jnp.int32, pairs[0][0].shape, 0)
    blocks = []
    for j in range(3):
        a, b = pairs[0][j], pairs[1][j]
        blocks.append(jnp.where(row < 12, a, turned(b, 12)))
        blocks.append(jnp.where(row < 12, turned(a, 12), b))
    return blocks


def blocks_of(value, n):
    return [value[72 * n + COLS * i : 72 * n + COLS * (i + 1)] for i in range(HALF)]


def set_bias(bias):
    last = (lax.axis_index("lat") == LAST_BAND).astype(jnp.int32)
    shape = (SPAN, GROUP * SPAN)
    for s in range(2):
        labels = []
        for dim in range(2):
            i = lax.broadcasted_iota(jnp.int32, shape, dim) % SPAN
            if s == 0:
                lat_row = i // COLS
                level = (i % COLS) // 12
            else:
                t = i % 72
                u = t % COLS
                lat_row = 2 * (t // COLS) + u // 12
                level = (u % 12) // 6
            labels.append((last * (lat_row < HALF).astype(jnp.int32), level))
        (kr, kl), (qr, ql) = labels
        same_row = kr == qr
        bias[s, 0] = jnp.where(same_row, 0.0, MASKED).astype(f32)
        bias[s, 1] = jnp.where(same_row & (kl == ql), 0.0, MASKED).astype(f32)


def norm_block(x, gain):
    mean = jnp.mean(x, axis=-1, keepdims=True)
    centered = x - mean
    inverse = lax.rsqrt(jnp.mean(centered * centered, axis=-1, keepdims=True) + 1e-05)
    xhat = centered * inverse
    return xhat, inverse, (xhat * gain).astype(bf16)


def load_windows(s, chunk_ref, gain_ref, normed, grads, xhat_ref, inverse_ref):
    gain = gain_ref[...]
    base = 2 * SPAN * s

    def store(off, xs, gs):
        x = jnp.concatenate(xs, axis=0)
        xhat, inverse, n = norm_block(x, gain)
        xhat_ref[base + off : base + off + 48] = xhat
        inverse_ref[base + off : base + off + 48] = jnp.broadcast_to(inverse, (48, LANES))
        normed[base + off : base + off + 48] = n
        grads[base + off : base + off + 48] = jnp.concatenate(gs, axis=0).astype(bf16)

    if s == 0:
        for p in range(2):
            halves = [chunk_ref(h, p)[...].astype(f32) for h in range(2)]
            xs = sum((blocks_of(v, 0) for v in halves), [])
            gs = sum((blocks_of(v, 1) for v in halves), [])
            for j in range(3):
                store(SPAN * p + 48 * j, xs[2 * j : 2 * j + 2], gs[2 * j : 2 * j + 2])
    else:
        parts = []
        for n in range(2):
            sides = []
            for kind in (2, 3):
                halves = [chunk_ref(h, kind)[...].astype(f32) for h in range(2)]
                sides.append(by_pair(sum((blocks_of(v, n) for v in halves), [])))
            parts.append([sides[0][p] + sides[1][p] for p in range(2)])
        for p in range(2):
            for j in range(3):
                store(
                    SPAN * p + 48 * j,
                    parts[0][p][2 * j : 2 * j + 2],
                    parts[1][p][2 * j : 2 * j + 2],
                )


def head_group(s, p, i, bias, qkv, d_attn, attn, d_qkv):
    rows = slice(SPAN * p, SPAN * (p + 1))
    base = 2 * SPAN * s + SPAN * p
    out_rows = slice(base, base + SPAN)

    def lanes(n):
        return slice(CH * n + GROUP_LANES * i, CH * n + GROUP_LANES * (i + 1))

    q, k, v = (qkv[rows, lanes(n)] for n in range(3))
    g = d_attn[rows, lanes(0)]
    head = lax.broadcasted_iota(jnp.int32, (SPAN, GROUP_LANES), 1) // HEAD_DIM
    zero = jnp.zeros((), bf16)

    def split(a):
        return jnp.concatenate([jnp.where(head == e, a, zero) for e in range(GROUP)], axis=0)

    def join(a):
        picked = a[:SPAN]
        for e in range(1, GROUP):
            picked = jnp.where(head == e, a[SPAN * e : SPAN * (e + 1)], picked)
        return picked

    qs, gs = split(q), split(g)
    scores = nt(k, qs) * (SCALE * LOG2E) + bias[s, p]
    top = jnp.max(scores, axis=0, keepdims=True)
    expo = jnp.exp2(scores - top)
    probs = expo * (1.0 / jnp.sum(expo, axis=0, keepdims=True))
    probs_b = probs.astype(bf16)
    d_probs = nt(v, gs)
    mean = jnp.sum(d_probs * probs, axis=0, keepdims=True)
    d_scores = (probs * (d_probs - mean)).astype(bf16)
    attn[out_rows, lanes(0)] = join(tn(probs_b, v)).astype(bf16)
    d_qkv[out_rows, lanes(0)] = (join(tn(d_scores, k)) * SCALE).astype(bf16)
    d_qkv[out_rows, lanes(1)] = (nn(d_scores, qs) * SCALE).astype(bf16)
    d_qkv[out_rows, lanes(2)] = nn(probs_b, gs).astype(bf16)


def windows_front(s, chunk_ref, w, scratch):
    w_qkv, w_out, gain_ref = w
    (normed, grads, attn, d_qkv, qkv, d_attn, xhat_ref, inverse_ref, branch, shifted, bias, gain_sum) = scratch
    base = 2 * SPAN * s
    rows = slice(base, base + 2 * SPAN)
    load_windows(s, chunk_ref, gain_ref, normed, grads, xhat_ref, inverse_ref)
    for n in range(3):
        cols = slice(CH * n, CH * (n + 1))
        qkv[:, cols] = nn(normed[rows], w_qkv[:, cols]).astype(bf16)
    d_attn[...] = nt(grads[rows], w_out[...]).astype(bf16)

    for i in range(HEADS // GROUP):
        for p in range(2):
            head_group(s, p, i, bias, qkv, d_attn, attn, d_qkv)


def windows_back(s, result_ref, w, scratch):
    w_qkv, w_out, gain_ref = w
    (normed, grads, attn, d_qkv, qkv, d_attn, xhat_ref, inverse_ref, branch, shifted, bias, gain_sum) = scratch
    base = 2 * SPAN * s
    rows = slice(base, base + 2 * SPAN)
    branch[...] = nn(attn[rows], w_out[...])
    shifted[...] = nt(d_qkv[rows], w_qkv[...])
    gain = gain_ref[...]
    for i in range(6):
        at = slice(48 * i, 48 * (i + 1))
        there = slice(base + 48 * i, base + 48 * (i + 1))
        d_normed = shifted[at]
        xhat = xhat_ref[there]
        gain_sum[...] += jnp.sum((d_normed * xhat).reshape(6, 8, CH), axis=0)
        d_xhat = d_normed * gain
        mean = jnp.mean(d_xhat, axis=-1, keepdims=True)
        slope = jnp.mean(d_xhat * xhat, axis=-1, keepdims=True)
        shifted[at] = inverse_ref[there, 0:1] * (d_xhat - mean - xhat * slope)
    if s == 0:
        for p in range(2):
            for h in range(2):
                at = slice(SPAN * p + 72 * h, SPAN * p + 72 * (h + 1))
                result_ref(h, p)[...] = jnp.concatenate(
                    [branch[at], shifted[at]], axis=0
                ).astype(bf16)
    else:
        for side, kind in enumerate((2, 3)):
            blocks = []
            for value in (branch, shifted):
                pairs = [
                    [
                        value[SPAN * p + 72 * side + COLS * j : SPAN * p + 72 * side + COLS * (j + 1)]
                        for j in range(3)
                    ]
                    for p in range(2)
                ]
                blocks.append(by_row(pairs))
            for h in range(2):
                result_ref(h, kind)[...] = jnp.concatenate(
                    blocks[0][HALF * h : HALF * h + HALF] + blocks[1][HALF * h : HALF * h + HALF],
                    axis=0,
                ).astype(bf16)


def weight_grads(n, total, scratch):
    normed, grads, attn, d_qkv = scratch[:4]
    cols = slice(CH * n, CH * (n + 1))
    if n < 3:
        total[:, cols] = tn(normed[...], d_qkv[:, cols]).astype(bf16)
    else:
        total[:, cols] = tn(attn[...], grads[...]).astype(bf16)


def gain_rows(gain_sum, gain_out):
    row = jnp.sum(gain_sum[...], axis=0, keepdims=True)
    gain_out[...] = jnp.concatenate(
        [row[:, LANES * i : LANES * (i + 1)] for i in range(4)] + [jnp.zeros((4, LANES), f32)],
        axis=0,
    )


WINDOW_SCRATCH = [
    pltpu.VMEM((4 * SPAN, CH), bf16),
    pltpu.VMEM((4 * SPAN, CH), bf16),
    pltpu.VMEM((4 * SPAN, CH), bf16),
    pltpu.VMEM((4 * SPAN, 3 * CH), bf16),
    pltpu.VMEM((2 * SPAN, 3 * CH), bf16),
    pltpu.VMEM((2 * SPAN, CH), bf16),
    pltpu.VMEM((4 * SPAN, CH), f32),
    pltpu.VMEM((4 * SPAN, LANES), f32),
    pltpu.VMEM((2 * SPAN, CH), f32),
    pltpu.VMEM((2 * SPAN, CH), f32),
    pltpu.VMEM((2, 2, SPAN, GROUP * SPAN), f32),
    pltpu.VMEM((8, CH), f32),
]


ORDER = (3, 0, 1, 2)
DIMS = (("x", "y"), ("y", "x"), ("x", "y"), ("y", "x"))


def partners():
    return (
        [along("core", 0)]
        + [along("x", k) for k in (1, 2, 3)]
        + [along("y", k) for k in (1, 2, 3)]
        + [along("z", k) for k in range(1, 8)]
    )


SUM_SCRATCH = [
    pltpu.VMEM((CH, GRADS), bf16),
    pltpu.VMEM((CH, GRADS), bf16),
    pltpu.VMEM((8, LANES), f32),
    pltpu.VMEM((256, GRADS), bf16),
    pltpu.VMEM((256, GRADS), bf16),
    pltpu.VMEM((4, 3, 64, CH), bf16),
    pltpu.VMEM((4, 64, CH), bf16),
    pltpu.VMEM((4, 7, 16, 256), bf16),
    pltpu.VMEM((4, 4, 16, 256), bf16),
    pltpu.VMEM((4, 8, 8, LANES), f32),
    pltpu.SemaphoreType.DMA((2, 4)),
    pltpu.SemaphoreType.DMA((2, 12)),
    pltpu.SemaphoreType.DMA((2, 28)),
    pltpu.SemaphoreType.DMA((2, 12)),
    pltpu.SemaphoreType.DMA((2, 14)),
    pltpu.SemaphoreType.DMA((2, 28)),
    pltpu.SemaphoreType.DMA((2, 12)),
    pltpu.SemaphoreType.DMA((2, 4)),
]

NEAR_LAST_4 = (2, 1, 3)
NEAR_LAST_8 = (4, 3, 5, 2, 6, 1, 7)


def ds(start, size):
    return pl.ds(pl.multiple_of(start, size), size)


class Sums:
    def __init__(self, gain_out, scratch):
        (self.total, self.out, self.gain_in, self.r0, self.b1, self.r1, self.b2, self.r2, self.ys, self.gs) = scratch[:10]
        sems = [(s.at[0], s.at[1]) for s in scratch[10:]]
        (self.s0, self.s1, self.s2, self.s3, self.sg, self.t2, self.t1, self.t0) = sems
        self.gain_out = gain_out
        x, y, z, core = place()
        self.at = {"x": x, "y": y, "z": z, "core": core}
        self.core = core
        self.started = []

    def go(self, copy):
        copy.start()
        self.started.append(copy)
        return copy

    def cols(self, j):
        n = ORDER[j]
        return slice(CH * n, CH * (n + 1))

    def core_send(self, j):
        cols = self.cols(j)
        theirs = ds((1 - self.core) * 256, 256)
        return self.go(
            send(self.total.at[theirs, cols], self.r0.at[:, cols], self.s0, j, along("core", 0))
        )

    def core_add(self, j):
        cols = self.cols(j)

        def step(i, _):
            here = ds(i * 64, 64)
            mine = ds(self.core * 256 + i * 64, 64)
            self.b1[here, cols] = (
                self.total[mine, cols].astype(f32) + self.r0[here, cols].astype(f32)
            ).astype(bf16)
            return 0

        lax.fori_loop(0, 4, step, 0)

    def first_send(self, j):
        d = DIMS[j][0]
        return [
            self.go(
                send(
                    self.b1.at[ds((self.at[d] + k) % 4 * 64, 64), self.cols(j)],
                    self.r1.at[j, k - 1],
                    self.s1,
                    3 * j + k - 1,
                    along(d, k),
                )
            )
            for k in NEAR_LAST_4
        ]

    def first_add(self, j):
        d = DIMS[j][0]

        def step(i, _):
            here = ds(i * 16, 16)
            mine = ds(self.at[d] * 64 + i * 16, 16)
            total = self.b1[mine, self.cols(j)].astype(f32)
            for k in range(3):
                total += self.r1[j, k, here].astype(f32)
            self.b2[j, here] = total.astype(bf16)
            return 0

        lax.fori_loop(0, 4, step, 0)

    def second_send(self, j):
        copies = []
        for k in NEAR_LAST_8:
            z = (self.at["z"] + k) % 8
            src = self.b2.at[j, ds(z // 2 * 16, 16), ds(z % 2 * 256, 256)]
            copies.append(
                self.go(send(src, self.r2.at[j, k - 1], self.s2, 7 * j + k - 1, along("z", k)))
            )
        return copies

    def second_add(self, j):
        z = self.at["z"]
        total = self.b2[j, ds(z // 2 * 16, 16), ds(z % 2 * 256, 256)].astype(f32)
        for k in range(7):
            total += self.r2[j, k].astype(f32)
        self.ys[j, self.at[DIMS[j][1]]] = total.astype(bf16)

    def third_send(self, j):
        d = DIMS[j][1]
        here = self.ys.at[j, self.at[d]]
        return [
            self.go(send(here, here, self.s3, 3 * j + k - 1, along(d, k))) for k in NEAR_LAST_4
        ]

    def piece(self, j, depth):
        start = self.core * 256
        if depth >= 1:
            start = start + self.at[DIMS[j][0]] * 64
        if depth < 2:
            return ds(start, (256, 64)[depth]), self.cols(j)
        z = self.at["z"]
        return ds(start + z // 2 * 16, 16), ds(CH * ORDER[j] + z % 2 * 256, 256)

    def third_add(self, j):
        total = self.ys[j, 0].astype(f32)
        for i in range(1, 4):
            total += self.ys[j, i].astype(f32)
        rows, cols = self.piece(j, 2)
        self.out[rows, cols] = total.astype(bf16)

    def spread(self, j, depth):
        rows, cols = self.piece(j, depth)
        here = self.out.at[rows, cols]
        dim, sems, first, near_last = (
            ("core", self.t0, j, (1,)),
            (DIMS[j][0], self.t1, 3 * j, NEAR_LAST_4),
            ("z", self.t2, 7 * j, NEAR_LAST_8),
        )[depth]
        return [self.go(send(here, here, sems, first + k - 1, along(dim, k))) for k in near_last]

    def gain_send(self, stage):
        dim, size, first = (("core", 2, 0), ("x", 4, 1), ("y", 4, 4), ("z", 8, 7))[stage]
        here = self.gs.at[stage, self.at[dim]]
        return [
            self.go(send(here, here, self.sg, first + k - 1, along(dim, k)))
            for k in range(1, size)
        ]

    def gain_add(self, stage, copies):
        for copy in copies:
            copy.wait_recv()
        total = self.gs[stage, 0]
        for i in range(1, (2, 4, 4, 8)[stage]):
            total = total + self.gs[stage, i]
        if stage == 3:
            self.gain_out[...] = total
        else:
            self.gs[stage + 1, self.at["xyz"[stage]]] = total


def arrived(copies):
    for copy in copies:
        copy.wait_recv()


ROUTES = ((0, 0, 1, 0), (0, 1, 1, 0), (0, 2, 1, 0), (0, 3, 1, 1), (1, 3, 0, 1))


def halo_neighbours():
    return [neighbour(s * a, s * b) for s in (1, -1) for a, b in ((1, 0), (0, 1), (1, 1))]


def layer_kernel(
    tokens_hbm, cotangent_hbm, w_qkv_hbm, w_out_hbm, gain,
    layer_out, grad_tokens, grad_qkv, grad_out, gain_out,
    packed, work, result, back, tokens, cotangent, layer_buf, grad_buf, w_qkv, w_out,
    in_sems, out_sems, copy_sems, *scratch,
):
    window_scratch, sum_scratch = scratch[: len(WINDOW_SCRATCH)], scratch[len(WINDOW_SCRATCH) :]
    tokens_in = []
    for h in range(2):
        rows = slice(HALF * h, HALF * (h + 1))
        for n, (src, dst) in enumerate(((tokens_hbm, tokens), (cotangent_hbm, cotangent))):
            tokens_in.append(
                pltpu.make_async_copy(src.at[:, rows], dst.at[:, rows], copy_sems.at[8 + 2 * h + n])
            )
            tokens_in[-1].start()
    weights_in = [
        pltpu.make_async_copy(w_qkv_hbm, w_qkv, copy_sems.at[0]),
        pltpu.make_async_copy(w_out_hbm, w_out, copy_sems.at[1]),
    ]
    for copy in weights_in:
        copy.start()
    greeted = halo_neighbours() + partners()
    greet(greeted)
    for copy in tokens_in[:2]:
        copy.wait()
    pack_half(0, tokens, cotangent, packed)
    pl.semaphore_wait(pltpu.get_barrier_semaphore(), len(greeted))
    inward = []
    for n, (h, kind, a, b) in enumerate(ROUTES):
        if n == 4:
            for copy in tokens_in[2:]:
                copy.wait()
            pack_half(1, tokens, cotangent, packed)
        copy = send(
            packed.at[h, kind], work.at[n], (in_sems.at[0], in_sems.at[1]), n, neighbour(-a, -b)
        )
        copy.start()
        inward.append(copy)

    def chunk_ref(h, kind):
        if h == 1 and kind < 3:
            return packed.at[1, kind]
        return work.at[4 if h == 1 else kind]

    sums = Sums(gain_out, sum_scratch)
    set_bias(window_scratch[10])
    window_scratch[11][...] = jnp.zeros((8, CH), f32)
    w = (w_qkv, w_out, gain)
    for copy in weights_in:
        copy.wait()
    def result_ref(h, kind):
        return result.at[h, kind]

    outward = []

    def send_back(numbers):
        for n in numbers:
            h, kind, a, b = ROUTES[n]
            copy = send(
                result.at[h, kind], back.at[n], (out_sems.at[0], out_sems.at[1]), n, neighbour(a, b)
            )
            copy.start()
            outward.append(copy)

    arrived(inward[0:2])
    windows_front(0, chunk_ref, w, window_scratch)
    windows_back(0, result_ref, w, window_scratch)
    send_back((0, 1))
    arrived(inward[2:5])
    windows_front(1, chunk_ref, w, window_scratch)

    by_core, first, second, third, spread2, spread1, spread0 = {}, {}, {}, {}, {}, {}, {}
    for j in range(4):
        weight_grads(ORDER[j], sums.total, window_scratch)
        by_core[j] = sums.core_send(j)
        if j >= 1:
            by_core[j - 1].wait_recv()
            sums.core_add(j - 1)
            first[j - 1] = sums.first_send(j - 1)
    by_core[3].wait_recv()
    sums.core_add(3)
    first[3] = sums.first_send(3)

    windows_back(1, result_ref, w, window_scratch)
    gain_rows(window_scratch[11], sums.gain_in)
    sums.gs[0, sums.core] = sums.gain_in[...]
    by_gain = sums.gain_send(0)
    for j in range(4):
        arrived(first[j])
        sums.first_add(j)
        second[j] = sums.second_send(j)
    send_back((3, 2, 4))
    sums.gain_add(0, by_gain)
    by_gain = sums.gain_send(1)
    for j in range(4):
        arrived(second[j])
        sums.second_add(j)
        third[j] = sums.third_send(j)
    sums.gain_add(1, by_gain)
    by_gain = sums.gain_send(2)
    for j in range(4):
        arrived(third[j])
        sums.third_add(j)
        spread2[j] = sums.spread(j, 2)
    sums.gain_add(2, by_gain)
    by_gain = sums.gain_send(3)

    arrived(outward)
    outputs = []
    for h in range(2):
        chunks = [back.at[n] for n in range(4)]
        if h == 1:
            chunks = [result.at[1, kind] for kind in range(3)] + [back.at[4]]
        unpack_half(h, chunks, tokens, cotangent, layer_buf, grad_buf)
        rows = slice(HALF * h, HALF * (h + 1))
        for n, (src, dst) in enumerate(((layer_buf, layer_out), (grad_buf, grad_tokens))):
            outputs.append(
                pltpu.make_async_copy(src.at[:, rows], dst.at[:, rows], copy_sems.at[12 + 2 * h + n])
            )
            outputs[-1].start()

    for j in range(4):
        arrived(spread2[j])
        spread1[j] = sums.spread(j, 1)
    sums.gain_add(3, by_gain)
    for j in range(4):
        arrived(spread1[j])
        spread0[j] = sums.spread(j, 0)
    for j in range(4):
        arrived(spread0[j])
        n = ORDER[j]
        cols = slice(CH * n, CH * (n + 1))
        outputs.append(
            pltpu.make_async_copy(
                sums.out.at[:, cols],
                grad_qkv.at[:, cols] if n < 3 else grad_out,
                copy_sems.at[4 + j],
            )
        )
        outputs[-1].start()
    for copy in inward + outward + sums.started:
        copy.wait_send()
    for copy in outputs:
        copy.wait()


def publish_kernel(*refs):
    inputs, outputs, sems = refs[:5], refs[5:10], refs[10]
    copies = [pltpu.make_async_copy(inputs[n], outputs[n], sems.at[n]) for n in range(4)]
    for copy in copies:
        copy.start()
    rows = inputs[4][...]
    outputs[4][...] = jnp.concatenate([rows[i : i + 1] for i in range(4)], axis=1)
    for copy in copies:
        copy.wait()


VMEM = pl.BlockSpec(memory_space=pltpu.VMEM)
ANY = pl.BlockSpec(memory_space=pl.ANY)
HBM = pl.BlockSpec(memory_space=pltpu.HBM)
LIMIT = 60 * 1024 * 1024


def local(tokens, cotangent, w_qkv, w_out, norm_gain_vector):
    shape = jax.ShapeDtypeStruct
    large = (
        shape(tokens.shape, bf16),
        shape(tokens.shape, bf16),
        shape((CH, 3 * CH), bf16),
        shape((CH, CH), bf16),
    )
    results = pl.pallas_call(
        layer_kernel,
        out_shape=large + (shape((8, LANES), f32),),
        in_specs=[HBM, HBM, HBM, HBM, VMEM],
        out_specs=(ANY, ANY, ANY, ANY, VMEM),
        scratch_shapes=[
            pltpu.VMEM((2, 4, CHUNK, CH), bf16),
            pltpu.VMEM((5, CHUNK, CH), bf16),
            pltpu.VMEM((2, 4, CHUNK, CH), bf16),
            pltpu.VMEM((5, CHUNK, CH), bf16),
            pltpu.VMEM(tokens.shape, bf16),
            pltpu.VMEM(tokens.shape, bf16),
            pltpu.VMEM(tokens.shape, bf16),
            pltpu.VMEM(tokens.shape, bf16),
            pltpu.VMEM((CH, 3 * CH), bf16),
            pltpu.VMEM((CH, CH), bf16),
            pltpu.SemaphoreType.DMA((2, 5)),
            pltpu.SemaphoreType.DMA((2, 5)),
            pltpu.SemaphoreType.DMA((16,)),
        ]
        + WINDOW_SCRATCH
        + SUM_SCRATCH,
        compiler_params=pltpu.CompilerParams(
            collective_id=0, has_side_effects=True, vmem_limit_bytes=LIMIT
        ),
    )(tokens, cotangent, w_qkv, w_out, norm_gain_vector.reshape(1, CH))
    layer_out, grad_tokens, grad_qkv, grad_out, gain_out = pl.pallas_call(
        publish_kernel,
        out_shape=large + (shape((1, CH), f32),),
        in_specs=[ANY, ANY, ANY, ANY, VMEM],
        out_specs=(HBM, HBM, HBM, HBM, VMEM),
        scratch_shapes=[pltpu.SemaphoreType.DMA((4,))],
        compiler_params=pltpu.CompilerParams(vmem_limit_bytes=8 * 1024 * 1024),
    )(*results)
    return (layer_out, grad_tokens, grad_qkv, grad_out, gain_out.reshape(CH))


def solution(mesh):
    return jax.shard_map(
        local,
        mesh=mesh,
        in_specs=(P(None, "lat", "lon", None), P(None, "lat", "lon", None), P(), P(), P()),
        out_specs=(P(None, "lat", "lon", None), P(None, "lat", "lon", None), P(), P(), P()),
        check_vma=False,
    )
```

```python
import functools

import jax
import jax.numpy as jnp
from jax import lax
from jax.experimental import pallas as pl
from jax.experimental.pallas import tpu as pltpu
from jax.sharding import PartitionSpec as P

CH = 512
HEADS = 8
HEAD_DIM = CH // HEADS
LEVELS = 4
ROWS = 6
HALF = 3
COLS = 24
SPAN = 144
CHUNK = 144
LAST_BAND = 7
GRADS = 4 * CH
SCALE = HEAD_DIM ** (-0.5)
LOG2E = 1.4426950408889634
MASKED = -1e30
LANES = 128
GROUP = 4
GROUP_LANES = GROUP * HEAD_DIM
MESH = pl.DeviceIdType.MESH
f32 = jnp.float32
bf16 = jnp.bfloat16


def nt(a, b):
    return lax.dot_general(a, b, (((1,), (1,)), ((), ())), preferred_element_type=f32)


def tn(a, b):
    return lax.dot_general(a, b, (((0,), (0,)), ((), ())), preferred_element_type=f32)


def nn(a, b):
    return lax.dot_general(a, b, (((1,), (0,)), ((), ())), preferred_element_type=f32)


def turned(v, by):
    by = by % COLS
    return v if by == 0 else pltpu.roll(v, by, axis=0)


def place():
    lat, lon = lax.axis_index("lat"), lax.axis_index("lon")
    y, x_hi = lat // 2, lat % 2
    x_lo, z, core = lon // 16, (lon % 16) // 2, lon % 2
    return 2 * x_hi + x_lo, y, z, core


def device_at(x, y, z, core):
    return (2 * y + x // 2, 16 * (x % 2) + 2 * z + core)


def neighbour(by_lat, by_lon):
    lat, lon = lax.axis_index("lat"), lax.axis_index("lon")
    return ((lat + by_lat + 8) % 8, (lon + by_lon + 32) % 32)


def along(dim, k):
    x, y, z, core = place()
    if dim == "x":
        return device_at((x + k) % 4, y, z, core)
    if dim == "y":
        return device_at(x, (y + k) % 4, z, core)
    if dim == "z":
        return device_at(x, y, (z + k) % 8, core)
    return device_at(x, y, z, 1 - core)


def send(src, dst, sems, slot, device):
    return pltpu.make_async_remote_copy(
        src_ref=src,
        dst_ref=dst,
        send_sem=sems[0].at[slot],
        recv_sem=sems[1].at[slot],
        device_id=device,
        device_id_type=MESH,
    )


def greet(devices):
    for device in devices:
        pl.semaphore_signal(
            pltpu.get_barrier_semaphore(), inc=1, device_id=device, device_id_type=MESH
        )


def pack_half(h, first, second, packed):
    row = lax.broadcasted_iota(jnp.int32, (COLS, LANES), 0)

    def lanes_step(c, _):
        lanes = pl.ds(pl.multiple_of(c * LANES, LANES), LANES)
        kinds = [[], [], [], []]
        for src in (first, second):
            for i in range(HALF):
                v0, v1, v2, v3 = (
                    src[l, HALF * h + i, :, lanes].astype(f32) for l in range(LEVELS)
                )
                kinds[0].append(jnp.where(row < 12, turned(v1, -6), turned(v2, 6)))
                kinds[1].append(jnp.where(row < 12, turned(v3, -6), turned(v0, 6)))
                kinds[2].append(
                    jnp.where(
                        row < 12,
                        jnp.where(row < 6, turned(v1, 6), turned(v2, 12)),
                        jnp.where(row < 18, turned(v3, 18), v0),
                    )
                )
                kinds[3].append(
                    jnp.where(
                        row < 12,
                        jnp.where(row < 6, v1, turned(v2, 6)),
                        jnp.where(row < 18, turned(v3, 12), turned(v0, 18)),
                    )
                )
        for kind in range(4):
            packed[h, kind, :, lanes] = jnp.concatenate(kinds[kind], axis=0).astype(bf16)
        return 0

    lax.fori_loop(0, CH // LANES, lanes_step, 0)


def unpack_half(h, chunks, first, second, first_out, second_out):
    row = lax.broadcasted_iota(jnp.int32, (COLS, LANES), 0)

    def lanes_step(c, _):
        lanes = pl.ds(pl.multiple_of(c * LANES, LANES), LANES)
        kinds = [chunks[kind][:, lanes].astype(f32) for kind in range(4)]
        for n, (src, out) in enumerate(((first, first_out), (second, second_out))):
            for i in range(HALF):
                at = 72 * n + COLS * i
                a0, a1, b, e = (kind[at : at + COLS] for kind in kinds)
                west, east = row < 6, row >= 18
                v1 = jnp.where(west, e, jnp.where(east, turned(b, 18), turned(a0, 6)))
                v2 = jnp.where(
                    west, turned(e, 18), jnp.where(east, turned(b, 12), turned(a0, 18))
                )
                v3 = jnp.where(
                    west, turned(e, 12), jnp.where(east, turned(b, 6), turned(a1, 6))
                )
                v0 = jnp.where(west, turned(e, 6), jnp.where(east, b, turned(a1, 18)))
                for l, v in enumerate((v0, v1, v2, v3)):
                    r = HALF * h + i
                    total = src[l, r, :, lanes].astype(f32) + v
                    out[l, r, :, lanes] = total.astype(bf16)
        return 0

    lax.fori_loop(0, CH // LANES, lanes_step, 0)


def by_pair(blocks):
    row = lax.broadcasted_iota(jnp.int32, blocks[0].shape, 0)
    pairs = ([], [])
    for j in range(3):
        a, b = blocks[2 * j], blocks[2 * j + 1]
        pairs[0].append(jnp.where(row < 12, a, turned(b, 12)))
        pairs[1].append(jnp.where(row < 12, turned(a, 12), b))
    return pairs


def by_row(pairs):
    row = lax.broadcasted_iota(jnp.int32, pairs[0][0].shape, 0)
    blocks = []
    for j in range(3):
        a, b = pairs[0][j], pairs[1][j]
        blocks.append(jnp.where(row < 12, a, turned(b, 12)))
        blocks.append(jnp.where(row < 12, turned(a, 12), b))
    return blocks


def blocks_of(value, n):
    return [value[72 * n + COLS * i : 72 * n + COLS * (i + 1)] for i in range(HALF)]


def set_bias(bias):
    last = (lax.axis_index("lat") == LAST_BAND).astype(jnp.int32)
    shape = (SPAN, GROUP * SPAN)
    for s in range(2):
        labels = []
        for dim in range(2):
            i = lax.broadcasted_iota(jnp.int32, shape, dim) % SPAN
            if s == 0:
                lat_row = i // COLS
                level = (i % COLS) // 12
            else:
                t = i % 72
                u = t % COLS
                lat_row = 2 * (t // COLS) + u // 12
                level = (u % 12) // 6
            labels.append((last * (lat_row < HALF).astype(jnp.int32), level))
        (kr, kl), (qr, ql) = labels
        same_row = kr == qr
        bias[s, 0] = jnp.where(same_row, 0.0, MASKED).astype(f32)
        bias[s, 1] = jnp.where(same_row & (kl == ql), 0.0, MASKED).astype(f32)


def norm_block(x, gain):
    mean = jnp.mean(x, axis=-1, keepdims=True)
    centered = x - mean
    inverse = lax.rsqrt(jnp.mean(centered * centered, axis=-1, keepdims=True) + 1e-05)
    xhat = centered * inverse
    return xhat, inverse, (xhat * gain).astype(bf16)


def load_windows(s, chunk_ref, gain_ref, normed, grads, xhat_ref, inverse_ref):
    gain = gain_ref[...]
    base = 2 * SPAN * s

    def store(off, xs, gs):
        x = jnp.concatenate(xs, axis=0)
        xhat, inverse, n = norm_block(x, gain)
        xhat_ref[base + off : base + off + 48] = xhat
        inverse_ref[base + off : base + off + 48] = jnp.broadcast_to(inverse, (48, LANES))
        normed[base + off : base + off + 48] = n
        grads[base + off : base + off + 48] = jnp.concatenate(gs, axis=0).astype(bf16)

    if s == 0:
        for p in range(2):
            halves = [chunk_ref(h, p)[...].astype(f32) for h in range(2)]
            xs = sum((blocks_of(v, 0) for v in halves), [])
            gs = sum((blocks_of(v, 1) for v in halves), [])
            for j in range(3):
                store(SPAN * p + 48 * j, xs[2 * j : 2 * j + 2], gs[2 * j : 2 * j + 2])
    else:
        parts = []
        for n in range(2):
            sides = []
            for kind in (2, 3):
                halves = [chunk_ref(h, kind)[...].astype(f32) for h in range(2)]
                sides.append(by_pair(sum((blocks_of(v, n) for v in halves), [])))
            parts.append([sides[0][p] + sides[1][p] for p in range(2)])
        for p in range(2):
            for j in range(3):
                store(
                    SPAN * p + 48 * j,
                    parts[0][p][2 * j : 2 * j + 2],
                    parts[1][p][2 * j : 2 * j + 2],
                )


def head_group(s, p, i, bias, qkv, d_attn, attn, d_qkv):
    rows = slice(SPAN * p, SPAN * (p + 1))
    base = 2 * SPAN * s + SPAN * p
    out_rows = slice(base, base + SPAN)

    def lanes(n):
        return slice(CH * n + GROUP_LANES * i, CH * n + GROUP_LANES * (i + 1))

    q, k, v = (qkv[rows, lanes(n)] for n in range(3))
    g = d_attn[rows, lanes(0)]
    head = lax.broadcasted_iota(jnp.int32, (SPAN, GROUP_LANES), 1) // HEAD_DIM
    zero = jnp.zeros((), bf16)

    def split(a):
        return jnp.concatenate([jnp.where(head == e, a, zero) for e in range(GROUP)], axis=0)

    def join(a):
        picked = a[:SPAN]
        for e in range(1, GROUP):
            picked = jnp.where(head == e, a[SPAN * e : SPAN * (e + 1)], picked)
        return picked

    qs, gs = split(q), split(g)
    scores = nt(k, qs) * (SCALE * LOG2E) + bias[s, p]
    top = jnp.max(scores, axis=0, keepdims=True)
    expo = jnp.exp2(scores - top)
    probs = expo * (1.0 / jnp.sum(expo, axis=0, keepdims=True))
    probs_b = probs.astype(bf16)
    d_probs = nt(v, gs)
    mean = jnp.sum(d_probs * probs, axis=0, keepdims=True)
    d_scores = (probs * (d_probs - mean)).astype(bf16)
    attn[out_rows, lanes(0)] = join(tn(probs_b, v)).astype(bf16)
    d_qkv[out_rows, lanes(0)] = (join(tn(d_scores, k)) * SCALE).astype(bf16)
    d_qkv[out_rows, lanes(1)] = (nn(d_scores, qs) * SCALE).astype(bf16)
    d_qkv[out_rows, lanes(2)] = nn(probs_b, gs).astype(bf16)


def windows_front(s, chunk_ref, w, scratch):
    w_qkv, w_out, gain_ref = w
    (normed, grads, attn, d_qkv, qkv, d_attn, xhat_ref, inverse_ref, branch, shifted, bias, gain_sum) = scratch
    base = 2 * SPAN * s
    rows = slice(base, base + 2 * SPAN)
    load_windows(s, chunk_ref, gain_ref, normed, grads, xhat_ref, inverse_ref)
    for n in range(3):
        cols = slice(CH * n, CH * (n + 1))
        qkv[:, cols] = nn(normed[rows], w_qkv[:, cols]).astype(bf16)
    d_attn[...] = nt(grads[rows], w_out[...]).astype(bf16)

    for i in range(HEADS // GROUP):
        for p in range(2):
            head_group(s, p, i, bias, qkv, d_attn, attn, d_qkv)


def windows_back(s, result_ref, w, scratch):
    w_qkv, w_out, gain_ref = w
    (normed, grads, attn, d_qkv, qkv, d_attn, xhat_ref, inverse_ref, branch, shifted, bias, gain_sum) = scratch
    base = 2 * SPAN * s
    rows = slice(base, base + 2 * SPAN)
    branch[...] = nn(attn[rows], w_out[...])
    shifted[...] = nt(d_qkv[rows], w_qkv[...])
    gain = gain_ref[...]
    for i in range(6):
        at = slice(48 * i, 48 * (i + 1))
        there = slice(base + 48 * i, base + 48 * (i + 1))
        d_normed = shifted[at]
        xhat = xhat_ref[there]
        gain_sum[...] += jnp.sum((d_normed * xhat).reshape(6, 8, CH), axis=0)
        d_xhat = d_normed * gain
        mean = jnp.mean(d_xhat, axis=-1, keepdims=True)
        slope = jnp.mean(d_xhat * xhat, axis=-1, keepdims=True)
        shifted[at] = inverse_ref[there, 0:1] * (d_xhat - mean - xhat * slope)
    if s == 0:
        for p in range(2):
            for h in range(2):
                at = slice(SPAN * p + 72 * h, SPAN * p + 72 * (h + 1))
                result_ref(h, p)[...] = jnp.concatenate(
                    [branch[at], shifted[at]], axis=0
                ).astype(bf16)
    else:
        for side, kind in enumerate((2, 3)):
            blocks = []
            for value in (branch, shifted):
                pairs = [
                    [
                        value[SPAN * p + 72 * side + COLS * j : SPAN * p + 72 * side + COLS * (j + 1)]
                        for j in range(3)
                    ]
                    for p in range(2)
                ]
                blocks.append(by_row(pairs))
            for h in range(2):
                result_ref(h, kind)[...] = jnp.concatenate(
                    blocks[0][HALF * h : HALF * h + HALF] + blocks[1][HALF * h : HALF * h + HALF],
                    axis=0,
                ).astype(bf16)


def weight_grads(n, total, scratch):
    normed, grads, attn, d_qkv = scratch[:4]
    cols = slice(CH * n, CH * (n + 1))
    if n < 3:
        total[:, cols] = tn(normed[...], d_qkv[:, cols]).astype(bf16)
    else:
        total[:, cols] = tn(attn[...], grads[...]).astype(bf16)


def gain_rows(gain_sum, gain_out):
    row = jnp.sum(gain_sum[...], axis=0, keepdims=True)
    gain_out[...] = jnp.concatenate(
        [row[:, LANES * i : LANES * (i + 1)] for i in range(4)] + [jnp.zeros((4, LANES), f32)],
        axis=0,
    )


WINDOW_SCRATCH = [
    pltpu.VMEM((4 * SPAN, CH), bf16),
    pltpu.VMEM((4 * SPAN, CH), bf16),
    pltpu.VMEM((4 * SPAN, CH), bf16),
    pltpu.VMEM((4 * SPAN, 3 * CH), bf16),
    pltpu.VMEM((2 * SPAN, 3 * CH), bf16),
    pltpu.VMEM((2 * SPAN, CH), bf16),
    pltpu.VMEM((4 * SPAN, CH), f32),
    pltpu.VMEM((4 * SPAN, LANES), f32),
    pltpu.VMEM((2 * SPAN, CH), f32),
    pltpu.VMEM((2 * SPAN, CH), f32),
    pltpu.VMEM((2, 2, SPAN, GROUP * SPAN), f32),
    pltpu.VMEM((8, CH), f32),
]


ORDER = (3, 0, 1, 2)
DIMS = (("x", "y"), ("y", "x"), ("x", "y"), ("y", "x"))


def partners():
    return (
        [along("core", 0)]
        + [along("x", k) for k in (1, 2, 3)]
        + [along("y", k) for k in (1, 2, 3)]
        + [along("z", k) for k in range(1, 8)]
    )


SUM_SCRATCH = [
    pltpu.VMEM((CH, GRADS), bf16),
    pltpu.VMEM((CH, GRADS), bf16),
    pltpu.VMEM((8, LANES), f32),
    pltpu.VMEM((256, GRADS), bf16),
    pltpu.VMEM((256, GRADS), bf16),
    pltpu.VMEM((4, 3, 64, CH), bf16),
    pltpu.VMEM((4, 64, CH), bf16),
    pltpu.VMEM((4, 7, 16, 256), bf16),
    pltpu.VMEM((4, 4, 16, 256), bf16),
    pltpu.VMEM((4, 8, 8, LANES), f32),
    pltpu.SemaphoreType.DMA((2, 4)),
    pltpu.SemaphoreType.DMA((2, 12)),
    pltpu.SemaphoreType.DMA((2, 28)),
    pltpu.SemaphoreType.DMA((2, 12)),
    pltpu.SemaphoreType.DMA((2, 14)),
    pltpu.SemaphoreType.DMA((2, 28)),
    pltpu.SemaphoreType.DMA((2, 12)),
    pltpu.SemaphoreType.DMA((2, 4)),
]

NEAR_LAST_4 = (2, 1, 3)
NEAR_LAST_8 = (4, 3, 5, 2, 6, 1, 7)


def ds(start, size):
    return pl.ds(pl.multiple_of(start, size), size)


class Sums:
    def __init__(self, gain_out, scratch):
        (self.total, self.out, self.gain_in, self.r0, self.b1, self.r1, self.b2, self.r2, self.ys, self.gs) = scratch[:10]
        sems = [(s.at[0], s.at[1]) for s in scratch[10:]]
        (self.s0, self.s1, self.s2, self.s3, self.sg, self.t2, self.t1, self.t0) = sems
        self.gain_out = gain_out
        x, y, z, core = place()
        self.at = {"x": x, "y": y, "z": z, "core": core}
        self.core = core
        self.started = []

    def go(self, copy):
        copy.start()
        self.started.append(copy)
        return copy

    def cols(self, j):
        n = ORDER[j]
        return slice(CH * n, CH * (n + 1))

    def core_send(self, j):
        cols = self.cols(j)
        theirs = ds((1 - self.core) * 256, 256)
        return self.go(
            send(self.total.at[theirs, cols], self.r0.at[:, cols], self.s0, j, along("core", 0))
        )

    def core_add(self, j):
        cols = self.cols(j)

        def step(i, _):
            here = ds(i * 64, 64)
            mine = ds(self.core * 256 + i * 64, 64)
            self.b1[here, cols] = (
                self.total[mine, cols].astype(f32) + self.r0[here, cols].astype(f32)
            ).astype(bf16)
            return 0

        lax.fori_loop(0, 4, step, 0)

    def first_send(self, j):
        d = DIMS[j][0]
        return [
            self.go(
                send(
                    self.b1.at[ds((self.at[d] + k) % 4 * 64, 64), self.cols(j)],
                    self.r1.at[j, k - 1],
                    self.s1,
                    3 * j + k - 1,
                    along(d, k),
                )
            )
            for k in NEAR_LAST_4
        ]

    def first_add(self, j):
        d = DIMS[j][0]

        def step(i, _):
            here = ds(i * 16, 16)
            mine = ds(self.at[d] * 64 + i * 16, 16)
            total = self.b1[mine, self.cols(j)].astype(f32)
            for k in range(3):
                total += self.r1[j, k, here].astype(f32)
            self.b2[j, here] = total.astype(bf16)
            return 0

        lax.fori_loop(0, 4, step, 0)

    def second_send(self, j):
        copies = []
        for k in NEAR_LAST_8:
            z = (self.at["z"] + k) % 8
            src = self.b2.at[j, ds(z // 2 * 16, 16), ds(z % 2 * 256, 256)]
            copies.append(
                self.go(send(src, self.r2.at[j, k - 1], self.s2, 7 * j + k - 1, along("z", k)))
            )
        return copies

    def second_add(self, j):
        z = self.at["z"]
        total = self.b2[j, ds(z // 2 * 16, 16), ds(z % 2 * 256, 256)].astype(f32)
        for k in range(7):
            total += self.r2[j, k].astype(f32)
        self.ys[j, self.at[DIMS[j][1]]] = total.astype(bf16)

    def third_send(self, j):
        d = DIMS[j][1]
        here = self.ys.at[j, self.at[d]]
        return [
            self.go(send(here, here, self.s3, 3 * j + k - 1, along(d, k))) for k in NEAR_LAST_4
        ]

    def piece(self, j, depth):
        start = self.core * 256
        if depth >= 1:
            start = start + self.at[DIMS[j][0]] * 64
        if depth < 2:
            return ds(start, (256, 64)[depth]), self.cols(j)
        z = self.at["z"]
        return ds(start + z // 2 * 16, 16), ds(CH * ORDER[j] + z % 2 * 256, 256)

    def third_add(self, j):
        total = self.ys[j, 0].astype(f32)
        for i in range(1, 4):
            total += self.ys[j, i].astype(f32)
        rows, cols = self.piece(j, 2)
        self.out[rows, cols] = total.astype(bf16)

    def spread(self, j, depth):
        rows, cols = self.piece(j, depth)
        here = self.out.at[rows, cols]
        dim, sems, first, near_last = (
            ("core", self.t0, j, (1,)),
            (DIMS[j][0], self.t1, 3 * j, NEAR_LAST_4),
            ("z", self.t2, 7 * j, NEAR_LAST_8),
        )[depth]
        return [self.go(send(here, here, sems, first + k - 1, along(dim, k))) for k in near_last]

    def gain_send(self, stage):
        dim, size, first = (("core", 2, 0), ("x", 4, 1), ("y", 4, 4), ("z", 8, 7))[stage]
        here = self.gs.at[stage, self.at[dim]]
        return [
            self.go(send(here, here, self.sg, first + k - 1, along(dim, k)))
            for k in range(1, size)
        ]

    def gain_add(self, stage, copies):
        for copy in copies:
            copy.wait_recv()
        total = self.gs[stage, 0]
        for i in range(1, (2, 4, 4, 8)[stage]):
            total = total + self.gs[stage, i]
        if stage == 3:
            self.gain_out[...] = total
        else:
            self.gs[stage + 1, self.at["xyz"[stage]]] = total


def arrived(copies):
    for copy in copies:
        copy.wait_recv()


ROUTES = ((0, 0, 1, 0), (0, 1, 1, 0), (0, 2, 1, 0), (0, 3, 1, 1), (1, 3, 0, 1))


def halo_neighbours():
    return [neighbour(s * a, s * b) for s in (1, -1) for a, b in ((1, 0), (0, 1), (1, 1))]


def layer_kernel(
    tokens_hbm, cotangent_hbm, w_qkv_hbm, w_out_hbm, gain,
    layer_out, grad_tokens, grad_qkv, grad_out, gain_out,
    packed, work, result, back, tokens, cotangent, layer_buf, grad_buf, w_qkv, w_out,
    in_sems, out_sems, copy_sems, *scratch,
):
    window_scratch, sum_scratch = scratch[: len(WINDOW_SCRATCH)], scratch[len(WINDOW_SCRATCH) :]
    tokens_in = []
    for h in range(2):
        rows = slice(HALF * h, HALF * (h + 1))
        for n, (src, dst) in enumerate(((tokens_hbm, tokens), (cotangent_hbm, cotangent))):
            tokens_in.append(
                pltpu.make_async_copy(src.at[:, rows], dst.at[:, rows], copy_sems.at[8 + 2 * h + n])
            )
            tokens_in[-1].start()
    weights_in = [
        pltpu.make_async_copy(w_qkv_hbm, w_qkv, copy_sems.at[0]),
        pltpu.make_async_copy(w_out_hbm, w_out, copy_sems.at[1]),
    ]
    for copy in weights_in:
        copy.start()
    greeted = halo_neighbours() + partners()
    greet(greeted)
    for copy in tokens_in[:2]:
        copy.wait()
    pack_half(0, tokens, cotangent, packed)
    pl.semaphore_wait(pltpu.get_barrier_semaphore(), len(greeted))
    inward = []
    for n, (h, kind, a, b) in enumerate(ROUTES):
        if n == 4:
            for copy in tokens_in[2:]:
                copy.wait()
            pack_half(1, tokens, cotangent, packed)
        copy = send(
            packed.at[h, kind], work.at[n], (in_sems.at[0], in_sems.at[1]), n, neighbour(-a, -b)
        )
        copy.start()
        inward.append(copy)

    def chunk_ref(h, kind):
        if h == 1 and kind < 3:
            return packed.at[1, kind]
        return work.at[4 if h == 1 else kind]

    sums = Sums(gain_out, sum_scratch)
    set_bias(window_scratch[10])
    window_scratch[11][...] = jnp.zeros((8, CH), f32)
    w = (w_qkv, w_out, gain)
    for copy in weights_in:
        copy.wait()
    def result_ref(h, kind):
        return result.at[h, kind]

    outward = []

    def send_back(numbers):
        for n in numbers:
            h, kind, a, b = ROUTES[n]
            copy = send(
                result.at[h, kind], back.at[n], (out_sems.at[0], out_sems.at[1]), n, neighbour(a, b)
            )
            copy.start()
            outward.append(copy)

    arrived(inward[0:2])
    windows_front(0, chunk_ref, w, window_scratch)
    windows_back(0, result_ref, w, window_scratch)
    send_back((0, 1))
    arrived(inward[2:5])
    windows_front(1, chunk_ref, w, window_scratch)

    by_core, first, second, third, spread2, spread1, spread0 = {}, {}, {}, {}, {}, {}, {}
    for j in range(4):
        weight_grads(ORDER[j], sums.total, window_scratch)
        by_core[j] = sums.core_send(j)
        if j >= 1:
            by_core[j - 1].wait_recv()
            sums.core_add(j - 1)
            first[j - 1] = sums.first_send(j - 1)
    by_core[3].wait_recv()
    sums.core_add(3)
    first[3] = sums.first_send(3)

    windows_back(1, result_ref, w, window_scratch)
    gain_rows(window_scratch[11], sums.gain_in)
    sums.gs[0, sums.core] = sums.gain_in[...]
    by_gain = sums.gain_send(0)
    for j in range(4):
        arrived(first[j])
        sums.first_add(j)
        second[j] = sums.second_send(j)
    send_back((3, 2, 4))
    sums.gain_add(0, by_gain)
    by_gain = sums.gain_send(1)
    for j in range(4):
        arrived(second[j])
        sums.second_add(j)
        third[j] = sums.third_send(j)
    sums.gain_add(1, by_gain)
    by_gain = sums.gain_send(2)
    for j in range(4):
        arrived(third[j])
        sums.third_add(j)
        spread2[j] = sums.spread(j, 2)
    sums.gain_add(2, by_gain)
    by_gain = sums.gain_send(3)

    arrived(outward)
    outputs = []
    for h in range(2):
        chunks = [back.at[n] for n in range(4)]
        if h == 1:
            chunks = [result.at[1, kind] for kind in range(3)] + [back.at[4]]
        unpack_half(h, chunks, tokens, cotangent, layer_buf, grad_buf)
        rows = slice(HALF * h, HALF * (h + 1))
        for n, (src, dst) in enumerate(((layer_buf, layer_out), (grad_buf, grad_tokens))):
            outputs.append(
                pltpu.make_async_copy(src.at[:, rows], dst.at[:, rows], copy_sems.at[12 + 2 * h + n])
            )
            outputs[-1].start()

    for j in range(4):
        arrived(spread2[j])
        spread1[j] = sums.spread(j, 1)
    sums.gain_add(3, by_gain)
    for j in range(4):
        arrived(spread1[j])
        spread0[j] = sums.spread(j, 0)
    for j in range(4):
        arrived(spread0[j])
        n = ORDER[j]
        cols = slice(CH * n, CH * (n + 1))
        outputs.append(
            pltpu.make_async_copy(
                sums.out.at[:, cols],
                grad_qkv.at[:, cols] if n < 3 else grad_out,
                copy_sems.at[4 + j],
            )
        )
        outputs[-1].start()
    for copy in inward + outward + sums.started:
        copy.wait_send()
    for copy in outputs:
        copy.wait()


def publish_kernel(*refs):
    inputs, outputs, bufs, sems = refs[:5], refs[5:10], refs[10:14], refs[14]
    reads = [pltpu.make_async_copy(inputs[n], bufs[n], sems.at[0, n]) for n in range(4)]
    writes = [pltpu.make_async_copy(bufs[n], outputs[n], sems.at[1, n]) for n in range(4)]
    for copy in reads:
        copy.start()
    rows = inputs[4][...]
    outputs[4][...] = jnp.concatenate([rows[i : i + 1] for i in range(4)], axis=1)
    for read, write in zip(reads, writes):
        read.wait()
        write.start()
    for copy in writes:
        copy.wait()


VMEM = pl.BlockSpec(memory_space=pltpu.VMEM)
ANY = pl.BlockSpec(memory_space=pl.ANY)
HBM = pl.BlockSpec(memory_space=pltpu.HBM)
LIMIT = 60 * 1024 * 1024


def local(tokens, cotangent, w_qkv, w_out, norm_gain_vector):
    shape = jax.ShapeDtypeStruct
    large = (
        shape(tokens.shape, bf16),
        shape(tokens.shape, bf16),
        shape((CH, 3 * CH), bf16),
        shape((CH, CH), bf16),
    )
    results = pl.pallas_call(
        layer_kernel,
        out_shape=large + (shape((8, LANES), f32),),
        in_specs=[HBM, HBM, HBM, HBM, VMEM],
        out_specs=(ANY, ANY, ANY, ANY, VMEM),
        scratch_shapes=[
            pltpu.VMEM((2, 4, CHUNK, CH), bf16),
            pltpu.VMEM((5, CHUNK, CH), bf16),
            pltpu.VMEM((2, 4, CHUNK, CH), bf16),
            pltpu.VMEM((5, CHUNK, CH), bf16),
            pltpu.VMEM(tokens.shape, bf16),
            pltpu.VMEM(tokens.shape, bf16),
            pltpu.VMEM(tokens.shape, bf16),
            pltpu.VMEM(tokens.shape, bf16),
            pltpu.VMEM((CH, 3 * CH), bf16),
            pltpu.VMEM((CH, CH), bf16),
            pltpu.SemaphoreType.DMA((2, 5)),
            pltpu.SemaphoreType.DMA((2, 5)),
            pltpu.SemaphoreType.DMA((16,)),
        ]
        + WINDOW_SCRATCH
        + SUM_SCRATCH,
        compiler_params=pltpu.CompilerParams(
            collective_id=0, has_side_effects=True, vmem_limit_bytes=LIMIT
        ),
    )(tokens, cotangent, w_qkv, w_out, norm_gain_vector.reshape(1, CH))
    layer_out, grad_tokens, grad_qkv, grad_out, gain_out = pl.pallas_call(
        publish_kernel,
        out_shape=large + (shape((1, CH), f32),),
        in_specs=[ANY, ANY, ANY, ANY, VMEM],
        out_specs=(HBM, HBM, HBM, HBM, VMEM),
        scratch_shapes=[pltpu.VMEM(a.shape, bf16) for a in large]
        + [pltpu.SemaphoreType.DMA((2, 4))],
        compiler_params=pltpu.CompilerParams(vmem_limit_bytes=LIMIT),
    )(*results)
    return (layer_out, grad_tokens, grad_qkv, grad_out, gain_out.reshape(CH))


def solution(mesh):
    return jax.shard_map(
        local,
        mesh=mesh,
        in_specs=(P(None, "lat", "lon", None), P(None, "lat", "lon", None), P(), P(), P()),
        out_specs=(P(None, "lat", "lon", None), P(None, "lat", "lon", None), P(), P(), P()),
        check_vma=False,
    )
```

```python
import functools

import jax
import jax.numpy as jnp
from jax import lax
from jax.experimental import pallas as pl
from jax.experimental.pallas import tpu as pltpu
from jax.sharding import PartitionSpec as P

CH = 512
HEADS = 8
HEAD_DIM = CH // HEADS
LEVELS = 4
ROWS = 6
HALF = 3
COLS = 24
SPAN = 144
CHUNK = 144
LAST_BAND = 7
GRADS = 4 * CH
SCALE = HEAD_DIM ** (-0.5)
LOG2E = 1.4426950408889634
MASKED = -1e30
LANES = 128
GROUP = 4
GROUP_LANES = GROUP * HEAD_DIM
MESH = pl.DeviceIdType.MESH
f32 = jnp.float32
bf16 = jnp.bfloat16


def nt(a, b):
    return lax.dot_general(a, b, (((1,), (1,)), ((), ())), preferred_element_type=f32)


def tn(a, b):
    return lax.dot_general(a, b, (((0,), (0,)), ((), ())), preferred_element_type=f32)


def nn(a, b):
    return lax.dot_general(a, b, (((1,), (0,)), ((), ())), preferred_element_type=f32)


def turned(v, by):
    by = by % COLS
    return v if by == 0 else pltpu.roll(v, by, axis=0)


def place():
    lat, lon = lax.axis_index("lat"), lax.axis_index("lon")
    y, x_hi = lat // 2, lat % 2
    x_lo, z, core = lon // 16, (lon % 16) // 2, lon % 2
    return 2 * x_hi + x_lo, y, z, core


def device_at(x, y, z, core):
    return (2 * y + x // 2, 16 * (x % 2) + 2 * z + core)


def neighbour(by_lat, by_lon):
    lat, lon = lax.axis_index("lat"), lax.axis_index("lon")
    return ((lat + by_lat + 8) % 8, (lon + by_lon + 32) % 32)


def along(dim, k):
    x, y, z, core = place()
    if dim == "x":
        return device_at((x + k) % 4, y, z, core)
    if dim == "y":
        return device_at(x, (y + k) % 4, z, core)
    if dim == "z":
        return device_at(x, y, (z + k) % 8, core)
    return device_at(x, y, z, 1 - core)


def send(src, dst, sems, slot, device):
    return pltpu.make_async_remote_copy(
        src_ref=src,
        dst_ref=dst,
        send_sem=sems[0].at[slot],
        recv_sem=sems[1].at[slot],
        device_id=device,
        device_id_type=MESH,
    )


def greet(devices):
    for device in devices:
        pl.semaphore_signal(
            pltpu.get_barrier_semaphore(), inc=1, device_id=device, device_id_type=MESH
        )


def pack_half(h, first, second, packed):
    row = lax.broadcasted_iota(jnp.int32, (COLS, LANES), 0)

    def lanes_step(c, _):
        lanes = pl.ds(pl.multiple_of(c * LANES, LANES), LANES)
        kinds = [[], [], [], []]
        for src in (first, second):
            for i in range(HALF):
                v0, v1, v2, v3 = (
                    src[l, HALF * h + i, :, lanes].astype(f32) for l in range(LEVELS)
                )
                kinds[0].append(jnp.where(row < 12, turned(v1, -6), turned(v2, 6)))
                kinds[1].append(jnp.where(row < 12, turned(v3, -6), turned(v0, 6)))
                kinds[2].append(
                    jnp.where(
                        row < 12,
                        jnp.where(row < 6, turned(v1, 6), turned(v2, 12)),
                        jnp.where(row < 18, turned(v3, 18), v0),
                    )
                )
                kinds[3].append(
                    jnp.where(
                        row < 12,
                        jnp.where(row < 6, v1, turned(v2, 6)),
                        jnp.where(row < 18, turned(v3, 12), turned(v0, 18)),
                    )
                )
        for kind in range(4):
            packed[h, kind, :, lanes] = jnp.concatenate(kinds[kind], axis=0).astype(bf16)
        return 0

    lax.fori_loop(0, CH // LANES, lanes_step, 0)


def unpack_half(h, chunks, first, second, first_out, second_out):
    row = lax.broadcasted_iota(jnp.int32, (COLS, LANES), 0)

    def lanes_step(c, _):
        lanes = pl.ds(pl.multiple_of(c * LANES, LANES), LANES)
        kinds = [chunks[kind][:, lanes].astype(f32) for kind in range(4)]
        for n, (src, out) in enumerate(((first, first_out), (second, second_out))):
            for i in range(HALF):
                at = 72 * n + COLS * i
                a0, a1, b, e = (kind[at : at + COLS] for kind in kinds)
                west, east = row < 6, row >= 18
                v1 = jnp.where(west, e, jnp.where(east, turned(b, 18), turned(a0, 6)))
                v2 = jnp.where(
                    west, turned(e, 18), jnp.where(east, turned(b, 12), turned(a0, 18))
                )
                v3 = jnp.where(
                    west, turned(e, 12), jnp.where(east, turned(b, 6), turned(a1, 6))
                )
                v0 = jnp.where(west, turned(e, 6), jnp.where(east, b, turned(a1, 18)))
                for l, v in enumerate((v0, v1, v2, v3)):
                    r = HALF * h + i
                    total = src[l, r, :, lanes].astype(f32) + v
                    out[l, r, :, lanes] = total.astype(bf16)
        return 0

    lax.fori_loop(0, CH // LANES, lanes_step, 0)


def by_pair(blocks):
    row = lax.broadcasted_iota(jnp.int32, blocks[0].shape, 0)
    pairs = ([], [])
    for j in range(3):
        a, b = blocks[2 * j], blocks[2 * j + 1]
        pairs[0].append(jnp.where(row < 12, a, turned(b, 12)))
        pairs[1].append(jnp.where(row < 12, turned(a, 12), b))
    return pairs


def by_row(pairs):
    row = lax.broadcasted_iota(jnp.int32, pairs[0][0].shape, 0)
    blocks = []
    for j in range(3):
        a, b = pairs[0][j], pairs[1][j]
        blocks.append(jnp.where(row < 12, a, turned(b, 12)))
        blocks.append(jnp.where(row < 12, turned(a, 12), b))
    return blocks


def blocks_of(value, n):
    return [value[72 * n + COLS * i : 72 * n + COLS * (i + 1)] for i in range(HALF)]


def set_bias(bias):
    last = (lax.axis_index("lat") == LAST_BAND).astype(jnp.int32)
    shape = (SPAN, GROUP * SPAN)
    for s in range(2):
        labels = []
        for dim in range(2):
            i = lax.broadcasted_iota(jnp.int32, shape, dim) % SPAN
            if s == 0:
                lat_row = i // COLS
                level = (i % COLS) // 12
            else:
                t = i % 72
                u = t % COLS
                lat_row = 2 * (t // COLS) + u // 12
                level = (u % 12) // 6
            labels.append((last * (lat_row < HALF).astype(jnp.int32), level))
        (kr, kl), (qr, ql) = labels
        same_row = kr == qr
        bias[s, 0] = jnp.where(same_row, 0.0, MASKED).astype(f32)
        bias[s, 1] = jnp.where(same_row & (kl == ql), 0.0, MASKED).astype(f32)


def norm_block(x, gain):
    mean = jnp.mean(x, axis=-1, keepdims=True)
    centered = x - mean
    inverse = lax.rsqrt(jnp.mean(centered * centered, axis=-1, keepdims=True) + 1e-05)
    xhat = centered * inverse
    return xhat, inverse, (xhat * gain).astype(bf16)


def load_windows(s, chunk_ref, gain_ref, normed, grads, xhat_ref, inverse_ref):
    gain = gain_ref[...]
    base = 2 * SPAN * s

    def store(off, xs, gs):
        x = jnp.concatenate(xs, axis=0)
        xhat, inverse, n = norm_block(x, gain)
        xhat_ref[base + off : base + off + 48] = xhat
        inverse_ref[base + off : base + off + 48] = jnp.broadcast_to(inverse, (48, LANES))
        normed[base + off : base + off + 48] = n
        grads[base + off : base + off + 48] = jnp.concatenate(gs, axis=0).astype(bf16)

    if s == 0:
        for p in range(2):
            halves = [chunk_ref(h, p)[...].astype(f32) for h in range(2)]
            xs = sum((blocks_of(v, 0) for v in halves), [])
            gs = sum((blocks_of(v, 1) for v in halves), [])
            for j in range(3):
                store(SPAN * p + 48 * j, xs[2 * j : 2 * j + 2], gs[2 * j : 2 * j + 2])
    else:
        parts = []
        for n in range(2):
            sides = []
            for kind in (2, 3):
                halves = [chunk_ref(h, kind)[...].astype(f32) for h in range(2)]
                sides.append(by_pair(sum((blocks_of(v, n) for v in halves), [])))
            parts.append([sides[0][p] + sides[1][p] for p in range(2)])
        for p in range(2):
            for j in range(3):
                store(
                    SPAN * p + 48 * j,
                    parts[0][p][2 * j : 2 * j + 2],
                    parts[1][p][2 * j : 2 * j + 2],
                )


def head_group(s, p, i, bias, qkv, d_attn, attn, d_qkv):
    rows = slice(SPAN * p, SPAN * (p + 1))
    base = 2 * SPAN * s + SPAN * p
    out_rows = slice(base, base + SPAN)

    def lanes(n):
        return slice(CH * n + GROUP_LANES * i, CH * n + GROUP_LANES * (i + 1))

    q, k, v = (qkv[rows, lanes(n)] for n in range(3))
    g = d_attn[rows, lanes(0)]
    head = lax.broadcasted_iota(jnp.int32, (SPAN, GROUP_LANES), 1) // HEAD_DIM
    zero = jnp.zeros((), bf16)

    def split(a):
        return jnp.concatenate([jnp.where(head == e, a, zero) for e in range(GROUP)], axis=0)

    def join(a):
        picked = a[:SPAN]
        for e in range(1, GROUP):
            picked = jnp.where(head == e, a[SPAN * e : SPAN * (e + 1)], picked)
        return picked

    qs, gs = split(q), split(g)
    scores = nt(k, qs) * (SCALE * LOG2E) + bias[s, p]
    top = jnp.max(scores, axis=0, keepdims=True)
    expo = jnp.exp2(scores - top)
    probs = expo * (1.0 / jnp.sum(expo, axis=0, keepdims=True))
    probs_b = probs.astype(bf16)
    d_probs = nt(v, gs)
    mean = jnp.sum(d_probs * probs, axis=0, keepdims=True)
    d_scores = (probs * (d_probs - mean)).astype(bf16)
    attn[out_rows, lanes(0)] = join(tn(probs_b, v)).astype(bf16)
    d_qkv[out_rows, lanes(0)] = (join(tn(d_scores, k)) * SCALE).astype(bf16)
    d_qkv[out_rows, lanes(1)] = (nn(d_scores, qs) * SCALE).astype(bf16)
    d_qkv[out_rows, lanes(2)] = nn(probs_b, gs).astype(bf16)


def windows_front(s, chunk_ref, w, scratch):
    w_qkv, w_out, gain_ref = w
    (normed, grads, attn, d_qkv, qkv, d_attn, xhat_ref, inverse_ref, branch, shifted, bias, gain_sum) = scratch
    base = 2 * SPAN * s
    rows = slice(base, base + 2 * SPAN)
    load_windows(s, chunk_ref, gain_ref, normed, grads, xhat_ref, inverse_ref)
    for n in range(3):
        cols = slice(CH * n, CH * (n + 1))
        qkv[:, cols] = nn(normed[rows], w_qkv[:, cols]).astype(bf16)
    d_attn[...] = nt(grads[rows], w_out[...]).astype(bf16)

    for i in range(HEADS // GROUP):
        for p in range(2):
            head_group(s, p, i, bias, qkv, d_attn, attn, d_qkv)


def windows_back(s, result_ref, w, scratch):
    w_qkv, w_out, gain_ref = w
    (normed, grads, attn, d_qkv, qkv, d_attn, xhat_ref, inverse_ref, branch, shifted, bias, gain_sum) = scratch
    base = 2 * SPAN * s
    rows = slice(base, base + 2 * SPAN)
    branch[...] = nn(attn[rows], w_out[...])
    shifted[...] = nt(d_qkv[rows], w_qkv[...])
    gain = gain_ref[...]
    for i in range(6):
        at = slice(48 * i, 48 * (i + 1))
        there = slice(base + 48 * i, base + 48 * (i + 1))
        d_normed = shifted[at]
        xhat = xhat_ref[there]
        gain_sum[...] += jnp.sum((d_normed * xhat).reshape(6, 8, CH), axis=0)
        d_xhat = d_normed * gain
        mean = jnp.mean(d_xhat, axis=-1, keepdims=True)
        slope = jnp.mean(d_xhat * xhat, axis=-1, keepdims=True)
        shifted[at] = inverse_ref[there, 0:1] * (d_xhat - mean - xhat * slope)
    if s == 0:
        for p in range(2):
            for h in range(2):
                at = slice(SPAN * p + 72 * h, SPAN * p + 72 * (h + 1))
                result_ref(h, p)[...] = jnp.concatenate(
                    [branch[at], shifted[at]], axis=0
                ).astype(bf16)
    else:
        for side, kind in enumerate((2, 3)):
            blocks = []
            for value in (branch, shifted):
                pairs = [
                    [
                        value[SPAN * p + 72 * side + COLS * j : SPAN * p + 72 * side + COLS * (j + 1)]
                        for j in range(3)
                    ]
                    for p in range(2)
                ]
                blocks.append(by_row(pairs))
            for h in range(2):
                result_ref(h, kind)[...] = jnp.concatenate(
                    blocks[0][HALF * h : HALF * h + HALF] + blocks[1][HALF * h : HALF * h + HALF],
                    axis=0,
                ).astype(bf16)


def weight_grads(n, total, scratch):
    normed, grads, attn, d_qkv = scratch[:4]
    cols = slice(CH * n, CH * (n + 1))
    if n < 3:
        total[:, cols] = tn(normed[...], d_qkv[:, cols]).astype(bf16)
    else:
        total[:, cols] = tn(attn[...], grads[...]).astype(bf16)


def gain_rows(gain_sum, gain_out):
    row = jnp.sum(gain_sum[...], axis=0, keepdims=True)
    gain_out[...] = jnp.concatenate(
        [row[:, LANES * i : LANES * (i + 1)] for i in range(4)] + [jnp.zeros((4, LANES), f32)],
        axis=0,
    )


WINDOW_SCRATCH = [
    pltpu.VMEM((4 * SPAN, CH), bf16),
    pltpu.VMEM((4 * SPAN, CH), bf16),
    pltpu.VMEM((4 * SPAN, CH), bf16),
    pltpu.VMEM((4 * SPAN, 3 * CH), bf16),
    pltpu.VMEM((2 * SPAN, 3 * CH), bf16),
    pltpu.VMEM((2 * SPAN, CH), bf16),
    pltpu.VMEM((4 * SPAN, CH), f32),
    pltpu.VMEM((4 * SPAN, LANES), f32),
    pltpu.VMEM((2 * SPAN, CH), f32),
    pltpu.VMEM((2 * SPAN, CH), f32),
    pltpu.VMEM((2, 2, SPAN, GROUP * SPAN), f32),
    pltpu.VMEM((8, CH), f32),
]


ORDER = (3, 0, 1, 2)
DIMS = (("x", "y"), ("y", "x"), ("x", "y"), ("y", "x"))


def partners():
    return (
        [along("core", 0)]
        + [along("x", k) for k in (1, 2, 3)]
        + [along("y", k) for k in (1, 2, 3)]
        + [along("z", k) for k in range(1, 8)]
    )


SUM_SCRATCH = [
    pltpu.VMEM((CH, GRADS), bf16),
    pltpu.VMEM((CH, GRADS), bf16),
    pltpu.VMEM((8, LANES), f32),
    pltpu.VMEM((256, GRADS), bf16),
    pltpu.VMEM((256, GRADS), bf16),
    pltpu.VMEM((4, 3, 64, CH), bf16),
    pltpu.VMEM((4, 64, CH), bf16),
    pltpu.VMEM((4, 7, 16, 256), bf16),
    pltpu.VMEM((4, 4, 16, 256), bf16),
    pltpu.VMEM((4, 8, 8, LANES), f32),
    pltpu.SemaphoreType.DMA((2, 4)),
    pltpu.SemaphoreType.DMA((2, 12)),
    pltpu.SemaphoreType.DMA((2, 28)),
    pltpu.SemaphoreType.DMA((2, 12)),
    pltpu.SemaphoreType.DMA((2, 14)),
    pltpu.SemaphoreType.DMA((2, 28)),
    pltpu.SemaphoreType.DMA((2, 12)),
    pltpu.SemaphoreType.DMA((2, 4)),
]

NEAR_LAST_4 = (2, 1, 3)
NEAR_LAST_8 = (4, 3, 5, 2, 6, 1, 7)


def ds(start, size):
    return pl.ds(pl.multiple_of(start, size), size)


class Sums:
    def __init__(self, gain_out, scratch):
        (self.total, self.out, self.gain_in, self.r0, self.b1, self.r1, self.b2, self.r2, self.ys, self.gs) = scratch[:10]
        sems = [(s.at[0], s.at[1]) for s in scratch[10:]]
        (self.s0, self.s1, self.s2, self.s3, self.sg, self.t2, self.t1, self.t0) = sems
        self.gain_out = gain_out
        x, y, z, core = place()
        self.at = {"x": x, "y": y, "z": z, "core": core}
        self.core = core
        self.started = []

    def go(self, copy):
        copy.start()
        self.started.append(copy)
        return copy

    def cols(self, j):
        n = ORDER[j]
        return slice(CH * n, CH * (n + 1))

    def core_send(self, j):
        cols = self.cols(j)
        theirs = ds((1 - self.core) * 256, 256)
        return self.go(
            send(self.total.at[theirs, cols], self.r0.at[:, cols], self.s0, j, along("core", 0))
        )

    def core_add(self, j):
        cols = self.cols(j)

        def step(i, _):
            here = ds(i * 64, 64)
            mine = ds(self.core * 256 + i * 64, 64)
            self.b1[here, cols] = (
                self.total[mine, cols].astype(f32) + self.r0[here, cols].astype(f32)
            ).astype(bf16)
            return 0

        lax.fori_loop(0, 4, step, 0)

    def first_send(self, j):
        d = DIMS[j][0]
        return [
            self.go(
                send(
                    self.b1.at[ds((self.at[d] + k) % 4 * 64, 64), self.cols(j)],
                    self.r1.at[j, k - 1],
                    self.s1,
                    3 * j + k - 1,
                    along(d, k),
                )
            )
            for k in NEAR_LAST_4
        ]

    def first_add(self, j):
        d = DIMS[j][0]

        def step(i, _):
            here = ds(i * 16, 16)
            mine = ds(self.at[d] * 64 + i * 16, 16)
            total = self.b1[mine, self.cols(j)].astype(f32)
            for k in range(3):
                total += self.r1[j, k, here].astype(f32)
            self.b2[j, here] = total.astype(bf16)
            return 0

        lax.fori_loop(0, 4, step, 0)

    def second_send(self, j):
        copies = []
        for k in NEAR_LAST_8:
            z = (self.at["z"] + k) % 8
            src = self.b2.at[j, ds(z // 2 * 16, 16), ds(z % 2 * 256, 256)]
            copies.append(
                self.go(send(src, self.r2.at[j, k - 1], self.s2, 7 * j + k - 1, along("z", k)))
            )
        return copies

    def second_add(self, j):
        z = self.at["z"]
        total = self.b2[j, ds(z // 2 * 16, 16), ds(z % 2 * 256, 256)].astype(f32)
        for k in range(7):
            total += self.r2[j, k].astype(f32)
        self.ys[j, self.at[DIMS[j][1]]] = total.astype(bf16)

    def third_send(self, j):
        d = DIMS[j][1]
        here = self.ys.at[j, self.at[d]]
        return [
            self.go(send(here, here, self.s3, 3 * j + k - 1, along(d, k))) for k in NEAR_LAST_4
        ]

    def piece(self, j, depth):
        start = self.core * 256
        if depth >= 1:
            start = start + self.at[DIMS[j][0]] * 64
        if depth < 2:
            return ds(start, (256, 64)[depth]), self.cols(j)
        z = self.at["z"]
        return ds(start + z // 2 * 16, 16), ds(CH * ORDER[j] + z % 2 * 256, 256)

    def third_add(self, j):
        total = self.ys[j, 0].astype(f32)
        for i in range(1, 4):
            total += self.ys[j, i].astype(f32)
        rows, cols = self.piece(j, 2)
        self.out[rows, cols] = total.astype(bf16)

    def spread(self, j, depth):
        rows, cols = self.piece(j, depth)
        here = self.out.at[rows, cols]
        dim, sems, first, near_last = (
            ("core", self.t0, j, (1,)),
            (DIMS[j][0], self.t1, 3 * j, NEAR_LAST_4),
            ("z", self.t2, 7 * j, NEAR_LAST_8),
        )[depth]
        return [self.go(send(here, here, sems, first + k - 1, along(dim, k))) for k in near_last]

    def gain_send(self, stage):
        dim, size, first = (("core", 2, 0), ("x", 4, 1), ("y", 4, 4), ("z", 8, 7))[stage]
        here = self.gs.at[stage, self.at[dim]]
        return [
            self.go(send(here, here, self.sg, first + k - 1, along(dim, k)))
            for k in range(1, size)
        ]

    def gain_add(self, stage, copies):
        for copy in copies:
            copy.wait_recv()
        total = self.gs[stage, 0]
        for i in range(1, (2, 4, 4, 8)[stage]):
            total = total + self.gs[stage, i]
        if stage == 3:
            self.gain_out[...] = total
        else:
            self.gs[stage + 1, self.at["xyz"[stage]]] = total


def arrived(copies):
    for copy in copies:
        copy.wait_recv()


ROUTES = ((0, 0, 1, 0), (0, 1, 1, 0), (0, 2, 1, 0), (0, 3, 1, 1), (1, 3, 0, 1))


def halo_neighbours():
    return [neighbour(s * a, s * b) for s in (1, -1) for a, b in ((1, 0), (0, 1), (1, 1))]


def layer_kernel(
    tokens_hbm, cotangent_hbm, w_qkv_hbm, w_out_hbm, gain,
    layer_out, grad_tokens, grad_qkv, grad_out, gain_out,
    packed, work, result, back, tokens, cotangent, layer_buf, grad_buf, w_qkv, w_out,
    in_sems, out_sems, copy_sems, *scratch,
):
    window_scratch, sum_scratch = scratch[: len(WINDOW_SCRATCH)], scratch[len(WINDOW_SCRATCH) :]
    tokens_in = []
    for h in range(2):
        rows = slice(HALF * h, HALF * (h + 1))
        for n, (src, dst) in enumerate(((tokens_hbm, tokens), (cotangent_hbm, cotangent))):
            tokens_in.append(
                pltpu.make_async_copy(src.at[:, rows], dst.at[:, rows], copy_sems.at[8 + 2 * h + n])
            )
            tokens_in[-1].start()
    weights_in = [
        pltpu.make_async_copy(w_qkv_hbm, w_qkv, copy_sems.at[0]),
        pltpu.make_async_copy(w_out_hbm, w_out, copy_sems.at[1]),
    ]
    for copy in weights_in:
        copy.start()
    greeted = halo_neighbours() + partners()
    greet(greeted)
    for copy in tokens_in[:2]:
        copy.wait()
    pack_half(0, tokens, cotangent, packed)
    pl.semaphore_wait(pltpu.get_barrier_semaphore(), len(greeted))
    inward = []
    for n, (h, kind, a, b) in enumerate(ROUTES):
        if n == 4:
            for copy in tokens_in[2:]:
                copy.wait()
            pack_half(1, tokens, cotangent, packed)
        copy = send(
            packed.at[h, kind], work.at[n], (in_sems.at[0], in_sems.at[1]), n, neighbour(-a, -b)
        )
        copy.start()
        inward.append(copy)

    def chunk_ref(h, kind):
        if h == 1 and kind < 3:
            return packed.at[1, kind]
        return work.at[4 if h == 1 else kind]

    sums = Sums(gain_out, sum_scratch)
    set_bias(window_scratch[10])
    window_scratch[11][...] = jnp.zeros((8, CH), f32)
    w = (w_qkv, w_out, gain)
    for copy in weights_in:
        copy.wait()
    def result_ref(h, kind):
        return result.at[h, kind]

    outward = []

    def send_back(numbers):
        for n in numbers:
            h, kind, a, b = ROUTES[n]
            copy = send(
                result.at[h, kind], back.at[n], (out_sems.at[0], out_sems.at[1]), n, neighbour(a, b)
            )
            copy.start()
            outward.append(copy)

    arrived(inward[0:2])
    windows_front(0, chunk_ref, w, window_scratch)
    windows_back(0, result_ref, w, window_scratch)
    send_back((0, 1))
    arrived(inward[2:5])
    windows_front(1, chunk_ref, w, window_scratch)

    by_core, first, second, third, spread2, spread1, spread0 = {}, {}, {}, {}, {}, {}, {}
    for j in range(4):
        weight_grads(ORDER[j], sums.total, window_scratch)
        by_core[j] = sums.core_send(j)
        if j >= 1:
            by_core[j - 1].wait_recv()
            sums.core_add(j - 1)
            first[j - 1] = sums.first_send(j - 1)
    by_core[3].wait_recv()
    sums.core_add(3)
    first[3] = sums.first_send(3)

    windows_back(1, result_ref, w, window_scratch)
    gain_rows(window_scratch[11], sums.gain_in)
    sums.gs[0, sums.core] = sums.gain_in[...]
    by_gain = sums.gain_send(0)
    for j in range(4):
        arrived(first[j])
        sums.first_add(j)
        second[j] = sums.second_send(j)
    sums.gain_add(0, by_gain)
    by_gain = sums.gain_send(1)
    for j in range(4):
        arrived(second[j])
        sums.second_add(j)
        third[j] = sums.third_send(j)
    send_back((3, 2, 4))
    sums.gain_add(1, by_gain)
    by_gain = sums.gain_send(2)
    for j in range(4):
        arrived(third[j])
        sums.third_add(j)
        spread2[j] = sums.spread(j, 2)
    sums.gain_add(2, by_gain)
    by_gain = sums.gain_send(3)

    arrived(outward)
    outputs = []
    for h in range(2):
        chunks = [back.at[n] for n in range(4)]
        if h == 1:
            chunks = [result.at[1, kind] for kind in range(3)] + [back.at[4]]
        unpack_half(h, chunks, tokens, cotangent, layer_buf, grad_buf)
        rows = slice(HALF * h, HALF * (h + 1))
        for n, (src, dst) in enumerate(((layer_buf, layer_out), (grad_buf, grad_tokens))):
            outputs.append(
                pltpu.make_async_copy(src.at[:, rows], dst.at[:, rows], copy_sems.at[12 + 2 * h + n])
            )
            outputs[-1].start()

    for j in range(4):
        arrived(spread2[j])
        spread1[j] = sums.spread(j, 1)
    sums.gain_add(3, by_gain)
    for j in range(4):
        arrived(spread1[j])
        spread0[j] = sums.spread(j, 0)
    for j in range(4):
        arrived(spread0[j])
        n = ORDER[j]
        cols = slice(CH * n, CH * (n + 1))
        outputs.append(
            pltpu.make_async_copy(
                sums.out.at[:, cols],
                grad_qkv.at[:, cols] if n < 3 else grad_out,
                copy_sems.at[4 + j],
            )
        )
        outputs[-1].start()
    for copy in inward + outward + sums.started:
        copy.wait_send()
    for copy in outputs:
        copy.wait()


def publish_kernel(*refs):
    inputs, outputs, bufs, sems = refs[:5], refs[5:10], refs[10:14], refs[14]
    reads = [pltpu.make_async_copy(inputs[n], bufs[n], sems.at[0, n]) for n in range(4)]
    writes = [pltpu.make_async_copy(bufs[n], outputs[n], sems.at[1, n]) for n in range(4)]
    for copy in reads:
        copy.start()
    rows = inputs[4][...]
    outputs[4][...] = jnp.concatenate([rows[i : i + 1] for i in range(4)], axis=1)
    for read, write in zip(reads, writes):
        read.wait()
        write.start()
    for copy in writes:
        copy.wait()


VMEM = pl.BlockSpec(memory_space=pltpu.VMEM)
ANY = pl.BlockSpec(memory_space=pl.ANY)
HBM = pl.BlockSpec(memory_space=pltpu.HBM)
LIMIT = 60 * 1024 * 1024


def local(tokens, cotangent, w_qkv, w_out, norm_gain_vector):
    shape = jax.ShapeDtypeStruct
    large = (
        shape(tokens.shape, bf16),
        shape(tokens.shape, bf16),
        shape((CH, 3 * CH), bf16),
        shape((CH, CH), bf16),
    )
    results = pl.pallas_call(
        layer_kernel,
        out_shape=large + (shape((8, LANES), f32),),
        in_specs=[HBM, HBM, HBM, HBM, VMEM],
        out_specs=(ANY, ANY, ANY, ANY, VMEM),
        scratch_shapes=[
            pltpu.VMEM((2, 4, CHUNK, CH), bf16),
            pltpu.VMEM((5, CHUNK, CH), bf16),
            pltpu.VMEM((2, 4, CHUNK, CH), bf16),
            pltpu.VMEM((5, CHUNK, CH), bf16),
            pltpu.VMEM(tokens.shape, bf16),
            pltpu.VMEM(tokens.shape, bf16),
            pltpu.VMEM(tokens.shape, bf16),
            pltpu.VMEM(tokens.shape, bf16),
            pltpu.VMEM((CH, 3 * CH), bf16),
            pltpu.VMEM((CH, CH), bf16),
            pltpu.SemaphoreType.DMA((2, 5)),
            pltpu.SemaphoreType.DMA((2, 5)),
            pltpu.SemaphoreType.DMA((16,)),
        ]
        + WINDOW_SCRATCH
        + SUM_SCRATCH,
        compiler_params=pltpu.CompilerParams(
            collective_id=0, has_side_effects=True, vmem_limit_bytes=LIMIT
        ),
    )(tokens, cotangent, w_qkv, w_out, norm_gain_vector.reshape(1, CH))
    layer_out, grad_tokens, grad_qkv, grad_out, gain_out = pl.pallas_call(
        publish_kernel,
        out_shape=large + (shape((1, CH), f32),),
        in_specs=[ANY, ANY, ANY, ANY, VMEM],
        out_specs=(HBM, HBM, HBM, HBM, VMEM),
        scratch_shapes=[pltpu.VMEM(a.shape, bf16) for a in large]
        + [pltpu.SemaphoreType.DMA((2, 4))],
        compiler_params=pltpu.CompilerParams(vmem_limit_bytes=LIMIT),
    )(*results)
    return (layer_out, grad_tokens, grad_qkv, grad_out, gain_out.reshape(CH))


def solution(mesh):
    return jax.shard_map(
        local,
        mesh=mesh,
        in_specs=(P(None, "lat", "lon", None), P(None, "lat", "lon", None), P(), P(), P()),
        out_specs=(P(None, "lat", "lon", None), P(None, "lat", "lon", None), P(), P(), P()),
        check_vma=False,
    )
```
